512 devices in a mesh: pipe: 8 (over x, core), rows: 64 (over y, z).
Axes of the slice: x: 4, y: 8, z: 8, core: 2. Of those that a mesh axis runs over, the one named last changes fastest.
Arguments:
- fwd_in: bfloat16 [8, 128, 512, 256], P('pipe', None, 'rows'), may hold values from -6 to 6
- bwd_in: bfloat16 [8, 128, 512, 256], P('pipe', None, 'rows'), may hold values from -6 to 6
- grad_in: bfloat16 [8, 128, 512, 256], P('pipe', None, 'rows'), may hold values from -6 to 6
- land_use: int32 [8, 2, 512, 256], P('pipe', None, 'rows'), may hold values from 0 to 7
- friction: float32 [8, 128, 8], P('pipe'), may hold values from 0.3 to 3
- weight_in: bfloat16 [8, 128, 1152], P('pipe'), may hold values from -0.1875 to 0.1875
- weight_out: bfloat16 [8, 128, 1152], P('pipe'), may hold values from -0.1875 to 0.1875
Outputs:
- handed_act: bfloat16 [8, 128, 512, 256], P('pipe', None, 'rows')
- handed_grad: bfloat16 [8, 128, 512, 256], P('pipe', None, 'rows')
- grad_w_in: float32 [8, 128, 1152], P('pipe')
- grad_w_out: float32 [8, 128, 1152], P('pipe')
The draws below stay inside these ranges and needn't reach their ends.
Inputs may be any that keep to these rules, and one draw needn't show every extreme that they name: `land_use`: land-use classes.
All inputs are finite; a program needn't handle non-finite values.
Results may differ from the reference program's by a relative error of at most 0.0038.
Values may be sent and summed in bfloat16 or wider, within the bound.
No kernel may reach another device: no remote copies, remote signals or barrier semaphores. Data moves between devices by JAX's collectives and lax.ppermute only.
A program may use at most 64 MiB of HBM per device.

```python
import math
import jax
import jax.numpy as jnp
from jax import lax

CH = 128
COLS = 256
CLASSES = 8
SECTIONS = 8
CROP_ROWS = 512


def place_ends(array, key, least, top_value):
    index_at = [jax.random.randint(jax.random.fold_in(key, axis), (), 0, length) for axis, length in enumerate(array.shape)]
    longest = array.shape.index(max(array.shape))
    neighbour = index_at[:longest] + [(index_at[longest] + 1) % array.shape[longest]] + index_at[longest + 1:]
    return array.at[tuple(index_at)].set(least).at[tuple(neighbour)].set(top_value)


def shard_levels(own_key, dims, cuts, smallest, top_value):
    level = 1.0
    for position, parts in cuts:
        heights = jax.random.uniform(jax.random.fold_in(jax.random.fold_in(own_key, 6), position), (parts,), jnp.float32, smallest / len(cuts), top_value / len(cuts))
        level = level * jnp.repeat(jnp.exp(heights), dims[position] // parts).reshape((-1,) + (1,) * (len(dims) - 1 - position))
    return level


def noise(rng, shape, spread, limit, split=(), held_as=jnp.bfloat16):
    level = shard_levels(rng, shape, split, -0.22, 0.18) if split else 1.0
    drawn = jax.random.normal(rng, shape, jnp.float32) * spread * level
    return jnp.minimum(jnp.maximum(drawn, -limit), limit).astype(held_as)


def setup_inputs(seed: int = 0) -> dict:
    splits = jax.random.split(jax.random.key(seed), 8)
    return {
        "fwd_in": noise(splits[0], (SECTIONS, CH, CROP_ROWS, COLS), 1.0, 6.0, ((0, 8), (2, 64))),
        "bwd_in": noise(splits[1], (SECTIONS, CH, CROP_ROWS, COLS), 1.0, 6.0, ((0, 8), (2, 64))),
        "grad_in": noise(splits[2], (SECTIONS, CH, CROP_ROWS, COLS), 1.0, 6.0, ((0, 8), (2, 64))),
        "land_use": place_ends(jax.random.randint(splits[3], (SECTIONS, 2, CROP_ROWS, COLS), 0, CLASSES), jax.random.fold_in(splits[3], 1), 0, CLASSES - 1).astype(jnp.int32),
        "friction": jnp.clip(jnp.exp(math.log(3.0) - 2.3025851 * jax.random.uniform(splits[4], (SECTIONS, CH, CLASSES), jnp.float32) ** shard_levels(splits[4], (SECTIONS, CH, CLASSES), ((0, 8),), -0.2, 0.2)), 0.3, 3.0),
        "weight_in": noise(splits[5], (SECTIONS, CH, 9 * CH), (9 * CH) ** -0.5, 0.1875, ((0, 8),)),
        "weight_out": noise(splits[6], (SECTIONS, CH, 9 * CH), (9 * CH) ** -0.5, 0.1875, ((0, 8),)),
    }


def conv_rows(padded, weight, out_rows):
    chans = padded.shape[0]
    cells = padded.shape[2]
    wide = jnp.pad(padded, ((0, 0), (0, 0), (1, 1)))
    total = jnp.zeros((weight.shape[0], out_rows, cells), jnp.float32)
    for offset_row in range(3):
        band = wide[:, offset_row:offset_row + out_rows, :]
        stacked = jnp.concatenate([band[:, :, offset_col:offset_col + cells] for offset_col in range(3)], axis=0)
        part_weight = weight[:, offset_row * 3 * chans:(offset_row + 1) * 3 * chans]
        total = total + jnp.einsum('ok,krw->orw', part_weight, stacked, preferred_element_type=jnp.float32)
    return total

def flipped(weight):
    outs_count = weight.shape[0]
    ins_count = weight.shape[1] // 9
    shaped = weight.reshape(outs_count, 9, ins_count)[:, ::-1, :]
    return jnp.transpose(shaped, (2, 1, 0)).reshape(ins_count, 9 * outs_count)

def weight_grad(grad, padded):
    cells = grad.shape[2]
    out_rows = grad.shape[1]
    wide = jnp.pad(padded, ((0, 0), (0, 0), (1, 1)))
    pieces = []
    for offset_row in range(3):
        band = wide[:, offset_row:offset_row + out_rows, :]
        stacked = jnp.concatenate([band[:, :, offset_col:offset_col + cells] for offset_col in range(3)], axis=0)
        pieces.append(jnp.einsum('orw,krw->ok', grad, stacked, preferred_element_type=jnp.float32))
    return jnp.concatenate(pieces, axis=1)

def friction_field(table, classes):
    levels = jnp.arange(table.shape[1], dtype=jnp.int32)
    onehot = (classes[None, :, :] == levels[:, None, None]).astype(jnp.float32)
    return jnp.einsum('ck,krw->crw', table, onehot, precision=lax.Precision.HIGHEST)

def pad_rows(field):
    return jnp.pad(field, ((0, 0), (1, 1), (0, 0)))

def one_section(pieces):
    forward_x, stored_x, grad_out, classes, table, first_w, second_w = pieces
    total_rows = forward_x.shape[1]
    cells = forward_x.shape[2]
    fric_fwd = friction_field(table, classes[0])
    hidden = conv_rows(pad_rows(forward_x), first_w, total_rows)
    active = (jax.nn.silu(hidden) * fric_fwd).astype(jnp.bfloat16)
    result = (forward_x.astype(jnp.float32) + conv_rows(pad_rows(active), second_w, total_rows)).astype(jnp.bfloat16)
    fric_bwd = friction_field(table, classes[1])
    hidden_b = conv_rows(pad_rows(stored_x), first_w, total_rows)
    sigma = jax.nn.sigmoid(hidden_b)
    active_b = (jax.nn.silu(hidden_b) * fric_bwd).astype(jnp.bfloat16)
    grad_act = conv_rows(pad_rows(grad_out), flipped(second_w), total_rows)
    grad_hidden = (grad_act * fric_bwd * (sigma * (1.0 + hidden_b * (1.0 - sigma)))).astype(jnp.bfloat16)
    grad_x = (grad_out.astype(jnp.float32) + conv_rows(pad_rows(grad_hidden), flipped(first_w), total_rows)).astype(jnp.bfloat16)
    unscale = 1.0 / jnp.sqrt(jnp.float32(total_rows * cells))
    grad_second = weight_grad(grad_out, pad_rows(active_b)) * unscale
    grad_first = weight_grad(grad_hidden, pad_rows(stored_x)) * unscale
    return (result, grad_x, grad_first, grad_second)

def reference(fwd_in, bwd_in, grad_in, land_use, friction, weight_in, weight_out):
    outputs, grads, grad_first, grad_second = lax.map(one_section, (fwd_in, bwd_in, grad_in, land_use, friction, weight_in, weight_out))
    zeros_one = jnp.zeros_like(outputs[:1])
    handed_act = jnp.concatenate([zeros_one, outputs[:-1]], axis=0)
    handed_grad = jnp.concatenate([grads[1:], zeros_one], axis=0)
    return (handed_act, handed_grad, grad_first, grad_second)
```

```python
import jax
import jax.numpy as jnp
from jax import lax
from jax.experimental import pallas as pl
from jax.experimental.pallas import tpu as pltpu
from jax.sharding import PartitionSpec as P

CH = 128
COLS = 256
LOCAL = 8
CLASSES = 8
TAPS = 9
WIDE = 3 * CH
HALO_ROWS = 6 * CH + 16
BF16 = jnp.bfloat16
F32 = jnp.float32
PARAMS = pltpu.CompilerParams(vmem_limit_bytes=56 * 1024 * 1024)


def pack_kernel(fwd_ref, bwd_ref, grad_ref, use_ref, head_ref, tail_ref):
    sub = lax.broadcasted_iota(jnp.int32, (16, COLS), 0)
    for i, ref in enumerate((fwd_ref, bwd_ref, grad_ref)):
        rows = jnp.swapaxes(ref[...], 0, 1)
        for k in range(2):
            head_ref[(2 * i + k) * CH : (2 * i + k + 1) * CH] = rows[k]
            tail_ref[(2 * i + k) * CH : (2 * i + k + 1) * CH] = rows[LOCAL - 2 + k]
    for ref, row in ((head_ref, 0), (tail_ref, LOCAL - 1)):
        first = use_ref[0, row : row + 1, :].astype(F32) + 1.0
        second = use_ref[1, row : row + 1, :].astype(F32) + 1.0
        both = jnp.where(sub == 0, first, jnp.where(sub == 1, second, 0.0))
        ref[6 * CH :] = both.astype(BF16)


def put_shifted(wide_ref, at, row):
    lane = lax.broadcasted_iota(jnp.int32, (CH, COLS), 1)
    zero = jnp.zeros((CH, COLS), BF16)
    wide_ref[at, 0:CH] = jnp.where(lane == 0, zero, pltpu.roll(row, 1, 1))
    wide_ref[at, CH : 2 * CH] = row
    wide_ref[at, 2 * CH :] = jnp.where(lane == COLS - 1, zero, pltpu.roll(row, COLS - 1, 1))


def three_rows(ref, at):
    return ref[pl.ds(at, 3)].reshape(-1, COLS)


def dot(a, b):
    return jnp.dot(a, b, preferred_element_type=F32)


def dot_cells(a, b):
    return lax.dot_general(a, b, (((1,), (1,)), ((), ())), preferred_element_type=F32)


def block_kernel(
    fwd_ref, bwd_ref, grad_ref, use_ref, above_ref, below_ref, table_ref, first_ref, second_ref,
    out_ref, gx_ref, gw_ref,
    rows_ref, wide_ref, wide_act_ref, wide_gh_ref, actb_ref, gh_ref, class_ref, flip1_ref, flip2_ref, res_ref,
):
    for t in range(TAPS):
        mirrored = (TAPS - 1 - t) * CH
        flip1_ref[:, mirrored : mirrored + CH] = first_ref[:, t * CH : (t + 1) * CH].T
        flip2_ref[:, mirrored : mirrored + CH] = second_ref[:, t * CH : (t + 1) * CH].T
    for i in range(2):
        class_ref[i, 0:1] = above_ref[6 * CH : 6 * CH + 16].astype(F32)[i : i + 1]
        class_ref[i, 9:10] = below_ref[6 * CH : 6 * CH + 16].astype(F32)[i : i + 1]
        class_ref[i, 1:9] = use_ref[i].astype(F32) + 1.0
    table = table_ref[...]
    high = table.astype(BF16).astype(F32)
    middle = (table - high).astype(BF16).astype(F32)
    low = table - high - middle
    terms = jnp.concatenate([high, middle, low], axis=1).astype(BF16)
    level = (lax.broadcasted_iota(jnp.int32, (3 * CLASSES, COLS), 0) % CLASSES + 1).astype(F32)

    def friction(i, r):
        onehot = jnp.where(class_ref[i, pl.ds(r, 1)] == level, 1.0, 0.0).astype(BF16)
        return dot(terms, onehot)

    for i, ref in enumerate((fwd_ref, bwd_ref, grad_ref)):
        rows_ref[i, 2:10] = jnp.swapaxes(ref[...], 0, 1)
        for k in range(2):
            rows_ref[i, k] = above_ref[(2 * i + k) * CH : (2 * i + k + 1) * CH]
            rows_ref[i, 10 + k] = below_ref[(2 * i + k) * CH : (2 * i + k + 1) * CH]

    def widen(r, carry):
        for i in range(3):
            put_shifted(wide_ref.at[i], r, rows_ref[i, r])
        return carry

    lax.fori_loop(0, 12, widen, 0, unroll=2)

    def hidden_rows(step, carry):
        for k in range(2):
            r = 2 * step + k
            h = dot(first_ref[...], three_rows(wide_ref.at[0], r))
            half = 0.5 * h
            act = (half + half * jnp.tanh(half)) * friction(0, r)
            put_shifted(wide_act_ref, r, act.astype(BF16))
            hb = dot(first_ref[...], three_rows(wide_ref.at[1], r))
            sig = 0.5 + 0.5 * jnp.tanh(0.5 * hb)
            fric = friction(1, r)
            actb_ref[r + 1] = (hb * sig * fric).astype(BF16)
            ga = dot(flip2_ref[...], three_rows(wide_ref.at[2], r))
            gh = (ga * fric * (sig * (1.0 + hb * (1.0 - sig)))).astype(BF16)
            gh_ref[r + 1] = gh
            put_shifted(wide_gh_ref, r, gh)
        return carry

    lax.fori_loop(0, 5, hidden_rows, 0)
    for ref in (actb_ref, gh_ref):
        for r in (0, 1, 10, 11):
            ref[r] = jnp.zeros((CH, COLS), BF16)

    def result_rows(step, carry):
        for k in range(4):
            r = 4 * step + k
            add = dot(second_ref[...], three_rows(wide_act_ref, r))
            res_ref[0, r] = (rows_ref[0, r + 2].astype(F32) + add).astype(BF16)
            add = dot(flip1_ref[...], three_rows(wide_gh_ref, r))
            res_ref[1, r] = (rows_ref[2, r + 2].astype(F32) + add).astype(BF16)
        return carry

    lax.fori_loop(0, 2, result_rows, 0)
    out_ref[...] = jnp.swapaxes(res_ref[0], 0, 1)
    gx_ref[...] = jnp.swapaxes(res_ref[1], 0, 1)

    total = None
    for r in range(10):
        part = dot_cells(three_rows(gh_ref, r), wide_ref[1, r + 1])
        total = part if total is None else total + part
    for a in range(3):
        for b in range(3):
            gw_ref[(a * 3 + b) * CH : (a * 3 + b + 1) * CH] = total[a * CH : (a + 1) * CH, b * CH : (b + 1) * CH].astype(BF16)
    total = None
    for r in range(10):
        part = dot_cells(wide_ref[2, r + 1], three_rows(actb_ref, r))
        total = part if total is None else total + part
    for a in range(3):
        for b in range(3):
            at = (TAPS + a * 3 + b) * CH
            gw_ref[at : at + CH] = total[a * CH : (a + 1) * CH, b * CH : (b + 1) * CH].astype(BF16)
    spare = gw_ref.shape[0] - 2 * TAPS * CH
    if spare:
        gw_ref[2 * TAPS * CH :] = jnp.zeros((spare, CH), BF16)


def sum_kernel(scale, parts_ref, out_ref):
    total = jnp.sum(parts_ref[...].astype(F32), axis=0) * scale
    out_ref[...] = jnp.broadcast_to(total.astype(BF16)[None], out_ref.shape)


def spread_kernel(flat_ref, first_ref, second_ref):
    for a in range(3):
        for b in range(3):
            at = (a * 3 + b) * CH
            to = ((2 - a) * 3 + b) * CH
            first_ref[:, to : to + CH] = flat_ref[at : at + CH].astype(F32)
            at = (TAPS + a * 3 + b) * CH
            to = (b * 3 + 2 - a) * CH
            second_ref[:, to : to + CH] = flat_ref[at : at + CH].astype(F32)


def body(fwd_in, bwd_in, grad_in, land_use, friction, weight_in, weight_out):
    shape = jax.ShapeDtypeStruct
    row_count = lax.axis_size("rows")
    sections = lax.axis_size("pipe")
    fwd, bwd, grad = fwd_in[0], bwd_in[0], grad_in[0]
    use, table, first, second = land_use[0], friction[0], weight_in[0], weight_out[0]
    share = -(-2 * TAPS * CH // (8 * row_count)) * 8
    scale = 1.0 / (LOCAL * row_count * COLS) ** 0.5

    head, tail = pl.pallas_call(
        pack_kernel, out_shape=(shape((HALO_ROWS, COLS), BF16),) * 2, compiler_params=PARAMS, name="pack_edges"
    )(fwd, bwd, grad, use)
    above = lax.ppermute(tail, "rows", [(i, i + 1) for i in range(row_count - 1)])
    below = lax.ppermute(head, "rows", [(i + 1, i) for i in range(row_count - 1)])
    result, grad_x, partial = pl.pallas_call(
        block_kernel,
        out_shape=(
            shape((CH, LOCAL, COLS), BF16),
            shape((CH, LOCAL, COLS), BF16),
            shape((row_count * share, CH), BF16),
        ),
        scratch_shapes=[
            pltpu.VMEM((3, 12, CH, COLS), BF16),
            pltpu.VMEM((3, 12, WIDE, COLS), BF16),
            pltpu.VMEM((10, WIDE, COLS), BF16),
            pltpu.VMEM((10, WIDE, COLS), BF16),
            pltpu.VMEM((12, CH, COLS), BF16),
            pltpu.VMEM((12, CH, COLS), BF16),
            pltpu.VMEM((2, 16, COLS), F32),
            pltpu.VMEM((CH, TAPS * CH), BF16),
            pltpu.VMEM((CH, TAPS * CH), BF16),
            pltpu.VMEM((2, LOCAL, CH, COLS), BF16),
        ],
        compiler_params=PARAMS,
        name="block",
    )(fwd, bwd, grad, use, above, below, table, first, second)
    handed_act = lax.ppermute(result, "pipe", [(i, i + 1) for i in range(sections - 1)])
    handed_grad = lax.ppermute(grad_x, "pipe", [(i + 1, i) for i in range(sections - 1)])
    shares = lax.all_to_all(partial.reshape(row_count, share, CH), "rows", 0, 0)
    summed = pl.pallas_call(
        lambda *refs: sum_kernel(scale, *refs),
        out_shape=shape((row_count, share, CH), BF16), compiler_params=PARAMS, name="sum_shares",
    )(shares)
    gathered = lax.all_to_all(summed, "rows", 0, 0).reshape(row_count * share, CH)
    grad_first, grad_second = pl.pallas_call(
        spread_kernel, out_shape=(shape((CH, TAPS * CH), F32),) * 2, compiler_params=PARAMS, name="spread"
    )(gathered)
    return (handed_act[None], handed_grad[None], grad_first[None], grad_second[None])


def solution(mesh):
    cells = P("pipe", None, "rows", None)
    own = P("pipe", None, None)
    return jax.shard_map(
        body,
        mesh=mesh,
        in_specs=(cells, cells, cells, cells, own, own, own),
        out_specs=(cells, cells, own, own),
        check_vma=False,
    )
```

```python
import jax
import jax.numpy as jnp
from jax import lax
from jax.experimental import pallas as pl
from jax.experimental.pallas import tpu as pltpu
from jax.sharding import PartitionSpec as P

CH = 128
COLS = 256
LOCAL = 8
CLASSES = 8
TAPS = 9
WIDE = 3 * CH
BF16 = jnp.bfloat16
F32 = jnp.float32


def fetch(sems, *pairs):
    copies = [pltpu.make_async_copy(src, dst, sems.at[i]) for i, (src, dst) in enumerate(pairs)]
    for copy in copies:
        copy.start()
    return copies


def edges_kernel(bwd_hbm, grad_hbm, fwd_hbm, use_hbm, head_ref, tail_ref, bwd_ref, grad_ref, fwd_ref, use_ref, sems):
    copies = fetch(sems, (bwd_hbm, bwd_ref), (grad_hbm, grad_ref), (fwd_hbm, fwd_ref), (use_hbm, use_ref))
    for i, ref in enumerate((bwd_ref, grad_ref, fwd_ref)):
        copies[i].wait()
        rows = jnp.swapaxes(ref[...], 0, 1)
        for k in range(2):
            head_ref[(2 * i + k) * CH : (2 * i + k + 1) * CH] = rows[k]
            tail_ref[(2 * i + k) * CH : (2 * i + k + 1) * CH] = rows[LOCAL - 2 + k]
    copies[3].wait()
    sub = lax.broadcasted_iota(jnp.int32, (16, COLS), 0)
    for out, edge in ((head_ref, 0), (tail_ref, LOCAL - 1)):
        ahead = use_ref[0, edge : edge + 1, :].astype(F32) + 1.0
        back = use_ref[1, edge : edge + 1, :].astype(F32) + 1.0
        out[6 * CH :] = jnp.where(sub == 0, ahead, jnp.where(sub == 1, back, 0.0)).astype(BF16)


def put_shifted(wide_ref, at, row):
    lane = lax.broadcasted_iota(jnp.int32, (CH, COLS), 1)
    zero = jnp.zeros((CH, COLS), BF16)
    wide_ref[at, 0:CH] = jnp.where(lane == 0, zero, pltpu.roll(row, 1, 1))
    wide_ref[at, CH : 2 * CH] = row
    wide_ref[at, 2 * CH :] = jnp.where(lane == COLS - 1, zero, pltpu.roll(row, COLS - 1, 1))


def three_rows(ref, at):
    return ref[pl.ds(at, 3)].reshape(-1, COLS)


def dot(a, b):
    return jnp.dot(a, b, preferred_element_type=F32)


def dot_cells(a, b):
    return lax.dot_general(a, b, (((1,), (1,)), ((), ())), preferred_element_type=F32)


def put_flipped(flip_ref, weight_ref):
    for t in range(TAPS):
        mirrored = (TAPS - 1 - t) * CH
        flip_ref[:, mirrored : mirrored + CH] = weight_ref[:, t * CH : (t + 1) * CH].T


def friction_terms(table):
    high = table.astype(BF16).astype(F32)
    middle = (table - high).astype(BF16).astype(F32)
    low = table - high - middle
    return jnp.concatenate([high, middle, low], axis=0).T.astype(BF16)


def friction_row(terms, classes):
    level = (lax.broadcasted_iota(jnp.int32, (3 * CLASSES, COLS), 0) % CLASSES + 1).astype(F32)
    return dot(terms, jnp.where(classes == level, 1.0, 0.0).astype(BF16))


def backward_row(first, flip2, fric, stored_rows, grad_rows):
    hb = dot(first, stored_rows)
    sig = 0.5 + 0.5 * jnp.tanh(0.5 * hb)
    active = (hb * sig * fric).astype(BF16)
    ga = dot(flip2, grad_rows)
    return active, (ga * fric * (sig * (1.0 + hb * (1.0 - sig)))).astype(BF16)


def inner_kernel(
    bwd_hbm, grad_hbm, use_hbm, table_hbm, first_hbm, second_hbm,
    gh_out_ref, near_ref, sum_ref, fric_ref, flip_ref,
    bwd_ref, grad_ref, use_ref, table_ref, first_ref, second_ref,
    wide_b_ref, wide_g_ref, actb_ref, gh_ref, class_ref, sems,
):
    copies = fetch(
        sems, (second_hbm, second_ref), (bwd_hbm, bwd_ref), (grad_hbm, grad_ref),
        (use_hbm, use_ref), (table_hbm, table_ref), (first_hbm, first_ref),
    )
    for ref in (actb_ref, gh_ref):
        for r in (0, 1, 8, 9):
            ref[r] = jnp.zeros((CH, COLS), BF16)
    copies[0].wait()
    put_flipped(flip_ref, second_ref)
    for i, (ref, wide_ref) in enumerate(((bwd_ref, wide_b_ref), (grad_ref, wide_g_ref))):
        copies[1 + i].wait()
        rows = jnp.swapaxes(ref[...], 0, 1)
        for r in range(LOCAL):
            put_shifted(wide_ref, r, rows[r])
        for k, r in enumerate((0, 1, LOCAL - 2, LOCAL - 1)):
            near_ref[i, k] = rows[r]
    copies[3].wait()
    copies[4].wait()
    class_ref[...] = use_ref[1].astype(F32) + 1.0
    terms = friction_terms(table_ref[...])
    for k, r in enumerate((0, LOCAL - 1)):
        fric_ref[k] = friction_row(terms, class_ref[r : r + 1])
    copies[5].wait()

    def step(n, carry):
        for k in range(3):
            r = 3 * n + k + 1
            active, gh = backward_row(
                first_ref[...], flip_ref[...], friction_row(terms, class_ref[pl.ds(r, 1)]),
                three_rows(wide_b_ref, r - 1), three_rows(wide_g_ref, r - 1),
            )
            actb_ref[r + 1] = active
            gh_ref[r + 1] = gh
            gh_out_ref[r - 1] = gh
        return carry

    lax.fori_loop(0, 2, step, 0)
    total = None
    for r in range(LOCAL):
        part = dot_cells(three_rows(gh_ref, r), wide_b_ref[r])
        total = part if total is None else total + part
    sum_ref[0] = total
    total = None
    for r in range(LOCAL):
        part = dot_cells(wide_g_ref[r], three_rows(actb_ref, r))
        total = part if total is None else total + part
    sum_ref[1] = total


def outer_kernel(
    first_hbm, near_ref, above_ref, below_ref, fric_ref, flip_ref, sum_ref,
    gh_out_ref, gw_ref,
    first_ref, wide_ref, sems,
):
    (copy,) = fetch(sems, (first_hbm, first_ref))
    for i in range(2):
        put_shifted(wide_ref.at[i], 0, above_ref[(2 * i + 1) * CH : (2 * i + 2) * CH])
        for k in range(4):
            put_shifted(wide_ref.at[i], 1 + k, near_ref[i, k])
        put_shifted(wide_ref.at[i], 5, below_ref[2 * i * CH : (2 * i + 1) * CH])
    copy.wait()
    first_part = second_part = None
    for k in range(2):
        stored_rows, grad_rows = three_rows(wide_ref.at[0], 3 * k), three_rows(wide_ref.at[1], 3 * k)
        active, gh = backward_row(first_ref[...], flip_ref[...], fric_ref[k], stored_rows, grad_rows)
        gh_out_ref[k] = gh
        one, two = dot_cells(gh, stored_rows), dot_cells(grad_rows, active)
        first_part = one if first_part is None else first_part + one
        second_part = two if second_part is None else second_part + two
    for a in range(3):
        for b in range(3):
            at = (a * 3 + b) * CH
            whole = sum_ref[0, a * CH : (a + 1) * CH, b * CH : (b + 1) * CH]
            whole = whole + first_part[:, (2 - a) * WIDE + b * CH : (2 - a) * WIDE + (b + 1) * CH]
            gw_ref[at : at + CH] = whole.astype(BF16)
            at = (TAPS + a * 3 + b) * CH
            whole = sum_ref[1, a * CH : (a + 1) * CH, b * CH : (b + 1) * CH]
            whole = whole + second_part[(2 - b) * WIDE + a * CH : (2 - b) * WIDE + (a + 1) * CH]
            gw_ref[at : at + CH] = whole.astype(BF16)
    spare = gw_ref.shape[0] - 2 * TAPS * CH
    if spare:
        gw_ref[2 * TAPS * CH :] = jnp.zeros((spare, CH), BF16)


def forward_kernel(
    fwd_hbm, use_hbm, table_hbm, first_hbm, second_hbm, above_ref, below_ref,
    out_ref,
    fwd_ref, use_ref, table_ref, first_ref, second_ref,
    rows_ref, wide_ref, wide_act_ref, class_ref, sems,
):
    copies = fetch(
        sems, (fwd_hbm, fwd_ref), (use_hbm, use_ref), (table_hbm, table_ref),
        (first_hbm, first_ref), (second_hbm, second_ref),
    )
    class_ref[0:1] = above_ref[6 * CH :].astype(F32)[0:1]
    class_ref[9:10] = below_ref[6 * CH :].astype(F32)[0:1]
    for k in range(2):
        put_shifted(wide_ref, k, above_ref[(4 + k) * CH : (5 + k) * CH])
        put_shifted(wide_ref, 10 + k, below_ref[(4 + k) * CH : (5 + k) * CH])
    copies[0].wait()
    rows = jnp.swapaxes(fwd_ref[...], 0, 1)
    rows_ref[...] = rows
    for r in range(LOCAL):
        put_shifted(wide_ref, 2 + r, rows[r])
    for copy in copies[1:]:
        copy.wait()
    class_ref[1:9] = use_ref[0].astype(F32) + 1.0
    terms = friction_terms(table_ref[...])

    def hidden_rows(step, carry):
        for k in range(5):
            r = 5 * step + k
            half = 0.5 * dot(first_ref[...], three_rows(wide_ref, r))
            act = (half + half * jnp.tanh(half)) * friction_row(terms, class_ref[pl.ds(r, 1)])
            put_shifted(wide_act_ref, r, act.astype(BF16))
        return carry

    lax.fori_loop(0, 2, hidden_rows, 0)

    def result_rows(step, carry):
        for k in range(4):
            r = 4 * step + k
            add = dot(second_ref[...], three_rows(wide_act_ref, r))
            out_ref[r] = (rows_ref[r].astype(F32) + add).astype(BF16)
        return carry

    lax.fori_loop(0, 2, result_rows, 0)


def grad_x_kernel(
    grad_hbm, first_hbm, table_hbm, inner_ref, outer_ref, near_ref, above_ref, below_ref, flip2_ref,
    gx_ref,
    grad_ref, first_ref, table_ref, rows_ref, wide_ref, beside_ref, flip_ref, sems,
):
    copies = fetch(sems, (first_hbm, first_ref), (table_hbm, table_ref), (grad_hbm, grad_ref))
    for i in range(2):
        for k in range(2):
            put_shifted(beside_ref.at[i], k, above_ref[(2 * i + k) * CH : (2 * i + k + 1) * CH])
            put_shifted(beside_ref.at[i], 4 + k, below_ref[(2 * i + k) * CH : (2 * i + k + 1) * CH])
        put_shifted(beside_ref.at[i], 2, near_ref[i, 0])
        put_shifted(beside_ref.at[i], 3, near_ref[i, 3])
    put_shifted(wide_ref, 1, outer_ref[0])
    for r in range(LOCAL - 2):
        put_shifted(wide_ref, 2 + r, inner_ref[r])
    put_shifted(wide_ref, 8, outer_ref[1])
    for copy in copies[:2]:
        copy.wait()
    put_flipped(flip_ref, first_ref)
    terms = friction_terms(table_ref[...])
    for k, ref in enumerate((above_ref, below_ref)):
        _, gh = backward_row(
            first_ref[...], flip2_ref[...], friction_row(terms, ref[6 * CH :].astype(F32)[1:2]),
            three_rows(beside_ref.at[0], 3 * k), three_rows(beside_ref.at[1], 3 * k),
        )
        put_shifted(wide_ref, 9 * k, gh)
    copies[2].wait()
    rows_ref[...] = jnp.swapaxes(grad_ref[...], 0, 1)

    def result_rows(step, carry):
        for k in range(4):
            r = 4 * step + k
            add = dot(flip_ref[...], three_rows(wide_ref, r))
            gx_ref[r] = (rows_ref[r].astype(F32) + add).astype(BF16)
        return carry

    lax.fori_loop(0, 2, result_rows, 0)


def turn_kernel(act_ref, grad_ref, act_out_ref, grad_out_ref):
    act_out_ref[...] = jnp.swapaxes(act_ref[...], 0, 1)
    grad_out_ref[...] = jnp.swapaxes(grad_ref[...], 0, 1)


def sum_kernel(scale, parts_ref, out_ref):
    total = jnp.sum(parts_ref[...].astype(F32), axis=0) * scale
    out_ref[...] = jnp.broadcast_to(total.astype(BF16)[None], out_ref.shape)


def spread_kernel(flat_ref, first_ref, second_ref):
    for a in range(3):
        for b in range(3):
            at = (a * 3 + b) * CH
            to = ((2 - a) * 3 + b) * CH
            first_ref[:, to : to + CH] = flat_ref[at : at + CH].astype(F32)
            at = (TAPS + a * 3 + b) * CH
            to = (b * 3 + 2 - a) * CH
            second_ref[:, to : to + CH] = flat_ref[at : at + CH].astype(F32)


def kernel_call(kernel, outs, scratch, name, flops, hbm, vmem, limit=24):
    outs = [jax.ShapeDtypeStruct(dims, kind) for dims, kind in outs]
    scratch = [(x.shape, x.dtype) for x in hbm] + scratch
    sems = [pltpu.SemaphoreType.DMA((len(hbm),))] if hbm else []
    size = sum(x.size * x.dtype.itemsize for x in [*hbm, *vmem, *outs])
    return pl.pallas_call(
        kernel,
        in_specs=[pl.BlockSpec(memory_space=pltpu.HBM)] * len(hbm) + [pl.BlockSpec(memory_space=pltpu.VMEM)] * len(vmem),
        out_shape=outs,
        scratch_shapes=[pltpu.VMEM(dims, kind) for dims, kind in scratch] + sems,
        cost_estimate=pl.CostEstimate(flops=flops, bytes_accessed=size, transcendentals=0),
        compiler_params=pltpu.CompilerParams(vmem_limit_bytes=limit * 1024 * 1024),
        name=name,
    )(*hbm, *vmem)


def body(fwd_in, bwd_in, grad_in, land_use, friction, weight_in, weight_out):
    row_count = lax.axis_size("rows")
    sections = lax.axis_size("pipe")
    fwd, bwd, grad = fwd_in[0], bwd_in[0], grad_in[0]
    use, table, first, second = land_use[0], friction[0].T, weight_in[0], weight_out[0]
    scale = 1.0 / (LOCAL * row_count * COLS) ** 0.5
    share = -(-2 * TAPS * CH // (8 * row_count)) * 8
    cells, weight = (CH, LOCAL, COLS), (CH, TAPS * CH)
    row, wide = (CH, COLS), (WIDE, COLS)
    row_flops = 2 * CH * TAPS * CH * COLS
    down = [(i, i + 1) for i in range(row_count - 1)]
    up = [(i + 1, i) for i in range(row_count - 1)]

    head, tail = kernel_call(
        edges_kernel, [((6 * CH + 16, COLS), BF16)] * 2, [], "edges", 0, [bwd, grad, fwd, use], [], 56
    )
    above, below = lax.ppermute(tail, "rows", down), lax.ppermute(head, "rows", up)
    gh_inner, near, sums, fric, flip = kernel_call(
        inner_kernel,
        [((LOCAL - 2, *row), BF16), ((2, 4, *row), BF16), ((2, WIDE, WIDE), F32), ((2, *row), F32), (weight, BF16)],
        [((LOCAL, *wide), BF16)] * 2 + [((10, *row), BF16)] * 2 + [((LOCAL, COLS), F32)],
        "inner", 28 * row_flops,
        [bwd, grad, use, table, first, second], [],
    )
    gh_outer, partial = kernel_call(
        outer_kernel,
        [((2, *row), BF16), ((row_count * share, CH), BF16)],
        [((2, 6, *wide), BF16)],
        "outer", 8 * row_flops,
        [first], [near, above, below, fric, flip, sums],
    )
    shares = lax.all_to_all(partial.reshape(row_count, share, CH), "rows", 0, 0)

    above, below, gh_outer = lax.optimization_barrier((above, below, gh_outer))
    (result,) = kernel_call(
        forward_kernel,
        [((LOCAL, *row), BF16)],
        [((LOCAL, *row), BF16), ((12, *wide), BF16), ((10, *wide), BF16), ((16, COLS), F32)],
        "forward", 18 * row_flops,
        [fwd, use, table, first, second], [above, below],
    )
    handed_act = lax.ppermute(result, "pipe", [(i, i + 1) for i in range(sections - 1)])
    (grad_x,) = kernel_call(
        grad_x_kernel,
        [((LOCAL, *row), BF16)],
        [((LOCAL, *row), BF16), ((10, *wide), BF16), ((2, 6, *wide), BF16), (weight, BF16)],
        "grad_x", 12 * row_flops,
        [grad, first, table], [gh_inner, gh_outer, near, above, below, flip],
    )
    handed_grad = lax.ppermute(grad_x, "pipe", [(i + 1, i) for i in range(sections - 1)])
    handed_act, handed_grad = kernel_call(
        turn_kernel, [(cells, BF16)] * 2, [], "turn", 0, [], [handed_act, handed_grad]
    )
    shares, result, grad_x = lax.optimization_barrier((shares, result, grad_x))

    (summed,) = kernel_call(
        lambda *refs: sum_kernel(scale, *refs), [((row_count, share, CH), BF16)], [], "sum_shares", 0, [], [shares]
    )
    gathered = lax.all_to_all(summed, "rows", 0, 0).reshape(row_count * share, CH)
    grad_first, grad_second = kernel_call(spread_kernel, [(weight, F32)] * 2, [], "spread", 0, [], [gathered])
    return (handed_act[None], handed_grad[None], grad_first[None], grad_second[None])


def solution(mesh):
    cells = P("pipe", None, "rows", None)
    own = P("pipe", None, None)
    return jax.shard_map(
        body,
        mesh=mesh,
        in_specs=(cells, cells, cells, cells, own, own, own),
        out_specs=(cells, cells, own, own),
        check_vma=False,
    )
```

```python
import jax
import jax.numpy as jnp
from jax import lax
from jax.experimental import pallas as pl
from jax.experimental.pallas import tpu as pltpu
from jax.sharding import PartitionSpec as P

CH = 128
COLS = 256
LOCAL = 8
CLASSES = 8
TAPS = 9
WIDE = 3 * CH
BF16 = jnp.bfloat16
F32 = jnp.float32


def fetch(sems, *pairs):
    copies = [pltpu.make_async_copy(src, dst, sems.at[i]) for i, (src, dst) in enumerate(pairs)]
    for copy in copies:
        copy.start()
    return copies


def edges_kernel(bwd_hbm, grad_hbm, fwd_hbm, use_hbm, head_ref, tail_ref, bwd_ref, grad_ref, fwd_ref, use_ref, sems):
    copies = fetch(sems, (bwd_hbm, bwd_ref), (grad_hbm, grad_ref), (fwd_hbm, fwd_ref), (use_hbm, use_ref))
    for i, ref in enumerate((bwd_ref, grad_ref, fwd_ref)):
        copies[i].wait()
        rows = jnp.swapaxes(ref[...], 0, 1)
        for k in range(2):
            head_ref[(2 * i + k) * CH : (2 * i + k + 1) * CH] = rows[k]
            tail_ref[(2 * i + k) * CH : (2 * i + k + 1) * CH] = rows[LOCAL - 2 + k]
    copies[3].wait()
    sub = lax.broadcasted_iota(jnp.int32, (16, COLS), 0)
    for out, edge in ((head_ref, 0), (tail_ref, LOCAL - 1)):
        ahead = use_ref[0, edge : edge + 1, :].astype(F32) + 1.0
        back = use_ref[1, edge : edge + 1, :].astype(F32) + 1.0
        out[6 * CH :] = jnp.where(sub == 0, ahead, jnp.where(sub == 1, back, 0.0)).astype(BF16)


def put_shifted(wide_ref, at, row):
    lane = lax.broadcasted_iota(jnp.int32, (CH, COLS), 1)
    zero = jnp.zeros((CH, COLS), BF16)
    wide_ref[at, 0:CH] = jnp.where(lane == 0, zero, pltpu.roll(row, 1, 1))
    wide_ref[at, CH : 2 * CH] = row
    wide_ref[at, 2 * CH :] = jnp.where(lane == COLS - 1, zero, pltpu.roll(row, COLS - 1, 1))


def three_rows(ref, at):
    return ref[pl.ds(at, 3)].reshape(-1, COLS)


def dot(a, b):
    return jnp.dot(a, b, preferred_element_type=F32)


def dot_cells(a, b):
    return lax.dot_general(a, b, (((1,), (1,)), ((), ())), preferred_element_type=F32)


def put_flipped(flip_ref, weight_ref):
    for t in range(TAPS):
        mirrored = (TAPS - 1 - t) * CH
        flip_ref[:, mirrored : mirrored + CH] = weight_ref[:, t * CH : (t + 1) * CH].T


def friction_terms(table):
    high = table.astype(BF16).astype(F32)
    middle = (table - high).astype(BF16).astype(F32)
    low = table - high - middle
    return jnp.concatenate([high, middle, low], axis=0).T.astype(BF16)


def friction_row(terms, classes):
    level = (lax.broadcasted_iota(jnp.int32, (3 * CLASSES, COLS), 0) % CLASSES + 1).astype(F32)
    return dot(terms, jnp.where(classes == level, 1.0, 0.0).astype(BF16))


def backward_row(first, flip2, fric, stored_rows, grad_rows):
    hb = dot(first, stored_rows)
    sig = 0.5 + 0.5 * jnp.tanh(0.5 * hb)
    active = (hb * sig * fric).astype(BF16)
    ga = dot(flip2, grad_rows)
    return active, (ga * fric * (sig * (1.0 + hb * (1.0 - sig)))).astype(BF16)


def inner_kernel(
    top_ref, bwd_ref, grad_ref, use_ref, table_ref, first_ref, second_ref,
    gh_out_ref, near_ref, sum_ref, fric_ref, flip_ref,
    wide_b_ref, wide_g_ref, actb_ref, gh_ref, class_ref,
):
    for ref in (actb_ref, gh_ref):
        for r in (0, 8, 9):
            ref[r] = jnp.zeros((CH, COLS), BF16)
    put_flipped(flip_ref, second_ref)
    for i, (ref, wide_ref) in enumerate(((bwd_ref, wide_b_ref), (grad_ref, wide_g_ref))):
        rows = jnp.swapaxes(ref[...], 0, 1)
        wide_ref[0] = jnp.zeros((WIDE, COLS), BF16)
        for r in range(LOCAL):
            put_shifted(wide_ref, r + 1, rows[r])
        for k, r in enumerate((0, 1, LOCAL - 2, LOCAL - 1)):
            near_ref[i, k] = rows[r]
    class_ref[...] = use_ref[1].astype(F32) + 1.0
    terms = friction_terms(table_ref[...])
    fric_ref[...] = friction_row(terms, class_ref[LOCAL - 1 : LOCAL])
    active, gh = backward_row(
        first_ref[...], flip_ref[...], friction_row(terms, class_ref[0:1] * top_ref[0]),
        three_rows(wide_b_ref, 0), three_rows(wide_g_ref, 0),
    )
    actb_ref[1] = active
    gh_ref[1] = gh

    def step(n, carry):
        for k in range(3):
            r = 3 * n + k + 1
            active, gh = backward_row(
                first_ref[...], flip_ref[...], friction_row(terms, class_ref[pl.ds(r, 1)]),
                three_rows(wide_b_ref, r), three_rows(wide_g_ref, r),
            )
            actb_ref[r + 1] = active
            gh_ref[r + 1] = gh
            gh_out_ref[r - 1] = gh
        return carry

    lax.fori_loop(0, 2, step, 0)
    total = None
    for r in range(LOCAL):
        part = dot_cells(three_rows(gh_ref, r), wide_b_ref[r + 1])
        total = part if total is None else total + part
    sum_ref[0] = total
    total = None
    for r in range(LOCAL):
        part = dot_cells(wide_g_ref[r + 1], three_rows(actb_ref, r))
        total = part if total is None else total + part
    sum_ref[1] = total


def outer_kernel(
    table_ref, first_ref, near_ref, below_ref, fric_ref, flip_ref, sum_ref,
    gh_out_ref, gw_ref,
    wide_ref,
):
    for i in range(2):
        for k in range(2):
            put_shifted(wide_ref.at[i], k, near_ref[i, 2 + k])
            put_shifted(wide_ref.at[i], 2 + k, below_ref[(2 * i + k) * CH : (2 * i + k + 1) * CH])
    last = friction_row(friction_terms(table_ref[...]), below_ref[6 * CH :].astype(F32)[1:2])
    first_part = second_part = None
    for k, fric in enumerate((fric_ref[...], last)):
        stored_rows, grad_rows = three_rows(wide_ref.at[0], k), three_rows(wide_ref.at[1], k)
        active, gh = backward_row(first_ref[...], flip_ref[...], fric, stored_rows, grad_rows)
        gh_out_ref[k] = gh
        one, two = dot_cells(gh, stored_rows), dot_cells(grad_rows, active)
        first_part = one if first_part is None else first_part + one
        second_part = two if second_part is None else second_part + two
    for a in range(3):
        for b in range(3):
            at = (a * 3 + b) * CH
            whole = sum_ref[0, a * CH : (a + 1) * CH, b * CH : (b + 1) * CH]
            whole = whole + first_part[:, (2 - a) * WIDE + b * CH : (2 - a) * WIDE + (b + 1) * CH]
            gw_ref[at : at + CH] = whole.astype(BF16)
            at = (TAPS + a * 3 + b) * CH
            whole = sum_ref[1, a * CH : (a + 1) * CH, b * CH : (b + 1) * CH]
            whole = whole + second_part[(2 - b) * WIDE + a * CH : (2 - b) * WIDE + (a + 1) * CH]
            gw_ref[at : at + CH] = whole.astype(BF16)
    spare = gw_ref.shape[0] - 2 * TAPS * CH
    if spare:
        gw_ref[2 * TAPS * CH :] = jnp.zeros((spare, CH), BF16)


def forward_kernel(
    fwd_ref, use_ref, table_ref, first_ref, second_ref, above_ref, below_ref,
    out_ref,
    rows_ref, wide_ref, wide_act_ref, class_ref,
):
    class_ref[0:1] = above_ref[6 * CH :].astype(F32)[0:1]
    class_ref[9:10] = below_ref[6 * CH :].astype(F32)[0:1]
    for k in range(2):
        put_shifted(wide_ref, k, above_ref[(4 + k) * CH : (5 + k) * CH])
        put_shifted(wide_ref, 10 + k, below_ref[(4 + k) * CH : (5 + k) * CH])
    rows = jnp.swapaxes(fwd_ref[...], 0, 1)
    rows_ref[...] = rows
    for r in range(LOCAL):
        put_shifted(wide_ref, 2 + r, rows[r])
    class_ref[1:9] = use_ref[0].astype(F32) + 1.0
    terms = friction_terms(table_ref[...])

    def hidden_rows(step, carry):
        for k in range(5):
            r = 5 * step + k
            half = 0.5 * dot(first_ref[...], three_rows(wide_ref, r))
            act = (half + half * jnp.tanh(half)) * friction_row(terms, class_ref[pl.ds(r, 1)])
            put_shifted(wide_act_ref, r, act.astype(BF16))
        return carry

    lax.fori_loop(0, 2, hidden_rows, 0)

    def result_rows(step, carry):
        for k in range(4):
            r = 4 * step + k
            add = dot(second_ref[...], three_rows(wide_act_ref, r))
            out_ref[r] = (rows_ref[r].astype(F32) + add).astype(BF16)
        return carry

    lax.fori_loop(0, 2, result_rows, 0)


def grad_x_kernel(
    use_ref, grad_ref, first_ref, table_ref, inner_ref, outer_ref, near_ref, above_ref, flip2_ref,
    gx_ref,
    rows_ref, wide_ref, beside_ref, flip_ref,
):
    for i in range(2):
        for k in range(2):
            put_shifted(beside_ref.at[i], k, above_ref[(2 * i + k) * CH : (2 * i + k + 1) * CH])
            put_shifted(beside_ref.at[i], 2 + k, near_ref[i, k])
    for r in range(LOCAL - 2):
        put_shifted(wide_ref, 2 + r, inner_ref[r])
    for k in range(2):
        put_shifted(wide_ref, 8 + k, outer_ref[k])
    put_flipped(flip_ref, first_ref)
    terms = friction_terms(table_ref[...])
    for k, classes in enumerate((above_ref[6 * CH :].astype(F32)[1:2], use_ref[1, 0:1].astype(F32) + 1.0)):
        _, gh = backward_row(
            first_ref[...], flip2_ref[...], friction_row(terms, classes),
            three_rows(beside_ref.at[0], k), three_rows(beside_ref.at[1], k),
        )
        put_shifted(wide_ref, k, gh)
    rows_ref[...] = jnp.swapaxes(grad_ref[...], 0, 1)

    def result_rows(step, carry):
        for k in range(4):
            r = 4 * step + k
            add = dot(flip_ref[...], three_rows(wide_ref, r))
            gx_ref[r] = (rows_ref[r].astype(F32) + add).astype(BF16)
        return carry

    lax.fori_loop(0, 2, result_rows, 0)


def turn_kernel(act_ref, grad_ref, act_out_ref, grad_out_ref):
    act_out_ref[...] = jnp.swapaxes(act_ref[...], 0, 1)
    grad_out_ref[...] = jnp.swapaxes(grad_ref[...], 0, 1)


def sum_kernel(scale, parts_ref, out_ref):
    total = jnp.sum(parts_ref[...].astype(F32), axis=0) * scale
    out_ref[...] = jnp.broadcast_to(total.astype(BF16)[None], out_ref.shape)


def spread_kernel(flat_ref, first_ref, second_ref):
    for a in range(3):
        for b in range(3):
            at = (a * 3 + b) * CH
            to = ((2 - a) * 3 + b) * CH
            first_ref[:, to : to + CH] = flat_ref[at : at + CH].astype(F32)
            at = (TAPS + a * 3 + b) * CH
            to = (b * 3 + 2 - a) * CH
            second_ref[:, to : to + CH] = flat_ref[at : at + CH].astype(F32)


def kernel_call(kernel, outs, scratch, name, flops, hbm, vmem, limit=24, smem=()):
    outs = [jax.ShapeDtypeStruct(dims, kind) for dims, kind in outs]
    scratch = [(x.shape, x.dtype) for x in hbm] + scratch
    sems = [pltpu.SemaphoreType.DMA((len(hbm),))] if hbm else []
    size = sum(x.size * x.dtype.itemsize for x in [*hbm, *vmem, *outs])
    spaces = [pltpu.SMEM] * len(smem) + [pltpu.HBM] * len(hbm) + [pltpu.VMEM] * len(vmem)
    return pl.pallas_call(
        kernel,
        in_specs=[pl.BlockSpec(memory_space=space) for space in spaces],
        out_shape=outs,
        scratch_shapes=[pltpu.VMEM(dims, kind) for dims, kind in scratch] + sems,
        cost_estimate=pl.CostEstimate(flops=flops, bytes_accessed=size, transcendentals=0),
        compiler_params=pltpu.CompilerParams(vmem_limit_bytes=limit * 1024 * 1024),
        name=name,
    )(*smem, *hbm, *vmem)


def body(fwd_in, bwd_in, grad_in, land_use, friction, weight_in, weight_out):
    row_count = lax.axis_size("rows")
    sections = lax.axis_size("pipe")
    fwd, bwd, grad = fwd_in[0], bwd_in[0], grad_in[0]
    use, table, first, second = land_use[0], friction[0].T, weight_in[0], weight_out[0]
    scale = 1.0 / (LOCAL * row_count * COLS) ** 0.5
    share = -(-2 * TAPS * CH // (8 * row_count)) * 8
    cells, weight = (CH, LOCAL, COLS), (CH, TAPS * CH)
    row, wide = (CH, COLS), (WIDE, COLS)
    row_flops = 2 * CH * TAPS * CH * COLS
    down = [(i, i + 1) for i in range(row_count - 1)]
    up = [(i + 1, i) for i in range(row_count - 1)]

    head, tail = kernel_call(
        edges_kernel, [((6 * CH + 16, COLS), BF16)] * 2, [], "edges", 0, [bwd, grad, fwd, use], [], 56
    )
    below, above = lax.ppermute(head, "rows", up), lax.ppermute(tail, "rows", down)
    top = (lax.axis_index("rows") == 0).astype(F32).reshape(1)
    gh_inner, near, sums, fric, flip = kernel_call(
        inner_kernel,
        [((LOCAL - 2, *row), BF16), ((2, 4, *row), BF16), ((2, WIDE, WIDE), F32), (row, F32), (weight, BF16)],
        [((LOCAL + 1, *wide), BF16)] * 2 + [((10, *row), BF16)] * 2 + [((LOCAL, COLS), F32)],
        "inner", 30 * row_flops,
        [], [bwd, grad, use, table, first, second], smem=[top],
    )
    gh_outer, partial = kernel_call(
        outer_kernel,
        [((2, *row), BF16), ((row_count * share, CH), BF16)],
        [((2, 4, *wide), BF16)],
        "outer", 8 * row_flops,
        [], [table, first, near, below, fric, flip, sums],
    )
    partial, above = lax.optimization_barrier((partial, above))
    shares = lax.all_to_all(partial.reshape(row_count, share, CH), "rows", 0, 0)

    fwd, gh_outer = lax.optimization_barrier((fwd, gh_outer))
    (result,) = kernel_call(
        forward_kernel,
        [((LOCAL, *row), BF16)],
        [((LOCAL, *row), BF16), ((12, *wide), BF16), ((10, *wide), BF16), ((16, COLS), F32)],
        "forward", 18 * row_flops,
        [], [fwd, use, table, first, second, above, below],
    )
    handed_act = lax.ppermute(result, "pipe", [(i, i + 1) for i in range(sections - 1)])
    (grad_x,) = kernel_call(
        grad_x_kernel,
        [((LOCAL, *row), BF16)],
        [((LOCAL, *row), BF16), ((10, *wide), BF16), ((2, 4, *wide), BF16), (weight, BF16)],
        "grad_x", 12 * row_flops,
        [], [use, grad, first, table, gh_inner, gh_outer, near, above, flip],
    )
    handed_grad = lax.ppermute(grad_x, "pipe", [(i + 1, i) for i in range(sections - 1)])
    handed_act, handed_grad = kernel_call(
        turn_kernel, [(cells, BF16)] * 2, [], "turn", 0, [], [handed_act, handed_grad]
    )
    shares, result, grad_x = lax.optimization_barrier((shares, result, grad_x))

    (summed,) = kernel_call(
        lambda *refs: sum_kernel(scale, *refs), [((row_count, share, CH), BF16)], [], "sum_shares", 0, [], [shares]
    )
    gathered = lax.all_to_all(summed, "rows", 0, 0).reshape(row_count * share, CH)
    grad_first, grad_second = kernel_call(spread_kernel, [(weight, F32)] * 2, [], "spread", 0, [], [gathered])
    return (handed_act[None], handed_grad[None], grad_first[None], grad_second[None])


def solution(mesh):
    cells = P("pipe", None, "rows", None)
    own = P("pipe", None, None)
    return jax.shard_map(
        body,
        mesh=mesh,
        in_specs=(cells, cells, cells, cells, own, own, own),
        out_specs=(cells, cells, own, own),
        check_vma=False,
    )
```

```python
import jax
import jax.numpy as jnp
from jax import lax
from jax.experimental import pallas as pl
from jax.experimental.pallas import tpu as pltpu
from jax.sharding import PartitionSpec as P

CH = 128
COLS = 256
LOCAL = 8
CLASSES = 8
TAPS = 9
WIDE = 3 * CH
BF16 = jnp.bfloat16
F32 = jnp.float32


def fetch(sems, *pairs):
    copies = [pltpu.make_async_copy(src, dst, sems.at[i]) for i, (src, dst) in enumerate(pairs)]
    for copy in copies:
        copy.start()
    return copies


def edges_kernel(bwd_hbm, grad_hbm, fwd_hbm, use_hbm, head_ref, tail_ref, bwd_ref, grad_ref, fwd_ref, use_ref, sems):
    copies = fetch(sems, (bwd_hbm, bwd_ref), (grad_hbm, grad_ref), (fwd_hbm, fwd_ref), (use_hbm, use_ref))
    for i, ref in enumerate((bwd_ref, grad_ref, fwd_ref)):
        copies[i].wait()
        rows = jnp.swapaxes(ref[...], 0, 1)
        for k in range(2):
            head_ref[(2 * i + k) * CH : (2 * i + k + 1) * CH] = rows[k]
            tail_ref[(2 * i + k) * CH : (2 * i + k + 1) * CH] = rows[LOCAL - 2 + k]
    copies[3].wait()
    sub = lax.broadcasted_iota(jnp.int32, (16, COLS), 0)
    for out, edge in ((head_ref, 0), (tail_ref, LOCAL - 1)):
        ahead = use_ref[0, edge : edge + 1, :].astype(F32) + 1.0
        back = use_ref[1, edge : edge + 1, :].astype(F32) + 1.0
        out[6 * CH :] = jnp.where(sub == 0, ahead, jnp.where(sub == 1, back, 0.0)).astype(BF16)


def put_shifted(wide_ref, at, row):
    lane = lax.broadcasted_iota(jnp.int32, (CH, COLS), 1)
    zero = jnp.zeros((CH, COLS), BF16)
    wide_ref[at, 0:CH] = jnp.where(lane == 0, zero, pltpu.roll(row, 1, 1))
    wide_ref[at, CH : 2 * CH] = row
    wide_ref[at, 2 * CH :] = jnp.where(lane == COLS - 1, zero, pltpu.roll(row, COLS - 1, 1))


def three_rows(ref, at):
    return ref[pl.ds(at, 3)].reshape(-1, COLS)


def dot(a, b):
    return jnp.dot(a, b, preferred_element_type=F32)


def dot_cells(a, b):
    return lax.dot_general(a, b, (((1,), (1,)), ((), ())), preferred_element_type=F32)


def put_flipped(flip_ref, weight_ref):
    for t in range(TAPS):
        mirrored = (TAPS - 1 - t) * CH
        flip_ref[:, mirrored : mirrored + CH] = weight_ref[:, t * CH : (t + 1) * CH].T


def friction_terms(table):
    high = table.astype(BF16).astype(F32)
    middle = (table - high).astype(BF16).astype(F32)
    low = table - high - middle
    return jnp.concatenate([high, middle, low], axis=0).T.astype(BF16)


def friction_row(terms, classes):
    level = (lax.broadcasted_iota(jnp.int32, (3 * CLASSES, COLS), 0) % CLASSES + 1).astype(F32)
    return dot(terms, jnp.where(classes == level, 1.0, 0.0).astype(BF16))


def backward_row(first, flip2, fric, stored_rows, grad_rows):
    hb = dot(first, stored_rows)
    sig = 0.5 + 0.5 * jnp.tanh(0.5 * hb)
    active = (hb * sig * fric).astype(BF16)
    ga = dot(flip2, grad_rows)
    return active, (ga * fric * (sig * (1.0 + hb * (1.0 - sig)))).astype(BF16)


def inner_kernel(
    top_ref, bwd_ref, grad_ref, use_ref, table_ref, first_ref, second_ref,
    gh_out_ref, near_ref, sum_ref, fric_ref, flip_ref,
    wide_b_ref, wide_g_ref, actb_ref, gh_ref, class_ref,
):
    for ref in (actb_ref, gh_ref):
        for r in (0, 8, 9):
            ref[r] = jnp.zeros((CH, COLS), BF16)
    put_flipped(flip_ref, second_ref)
    for i, (ref, wide_ref) in enumerate(((bwd_ref, wide_b_ref), (grad_ref, wide_g_ref))):
        rows = jnp.swapaxes(ref[...], 0, 1)
        wide_ref[0] = jnp.zeros((WIDE, COLS), BF16)
        for r in range(LOCAL):
            put_shifted(wide_ref, r + 1, rows[r])
        for k, r in enumerate((0, 1, LOCAL - 2, LOCAL - 1)):
            near_ref[i, k] = rows[r]
    class_ref[...] = use_ref[1].astype(F32) + 1.0
    terms = friction_terms(table_ref[...])
    fric_ref[...] = friction_row(terms, class_ref[LOCAL - 1 : LOCAL])
    active, gh = backward_row(
        first_ref[...], flip_ref[...], friction_row(terms, class_ref[0:1] * top_ref[0]),
        three_rows(wide_b_ref, 0), three_rows(wide_g_ref, 0),
    )
    actb_ref[1] = active
    gh_ref[1] = gh

    def step(n, carry):
        for k in range(3):
            r = 3 * n + k + 1
            active, gh = backward_row(
                first_ref[...], flip_ref[...], friction_row(terms, class_ref[pl.ds(r, 1)]),
                three_rows(wide_b_ref, r), three_rows(wide_g_ref, r),
            )
            actb_ref[r + 1] = active
            gh_ref[r + 1] = gh
            gh_out_ref[r - 1] = gh
        return carry

    lax.fori_loop(0, 2, step, 0)
    total = None
    for r in range(LOCAL):
        part = dot_cells(three_rows(gh_ref, r), wide_b_ref[r + 1])
        total = part if total is None else total + part
    sum_ref[0] = total
    total = None
    for r in range(LOCAL):
        part = dot_cells(wide_g_ref[r + 1], three_rows(actb_ref, r))
        total = part if total is None else total + part
    sum_ref[1] = total


def outer_kernel(
    table_ref, first_ref, near_ref, below_ref, fric_ref, flip_ref, sum_ref,
    gh_out_ref, gw_ref,
    wide_ref,
):
    for i in range(2):
        for k in range(2):
            put_shifted(wide_ref.at[i], k, near_ref[i, 2 + k])
            put_shifted(wide_ref.at[i], 2 + k, below_ref[(2 * i + k) * CH : (2 * i + k + 1) * CH])
    last = friction_row(friction_terms(table_ref[...]), below_ref[6 * CH :].astype(F32)[1:2])
    first_part = second_part = None
    for k, fric in enumerate((fric_ref[...], last)):
        stored_rows, grad_rows = three_rows(wide_ref.at[0], k), three_rows(wide_ref.at[1], k)
        active, gh = backward_row(first_ref[...], flip_ref[...], fric, stored_rows, grad_rows)
        gh_out_ref[k] = gh
        one, two = dot_cells(gh, stored_rows), dot_cells(grad_rows, active)
        first_part = one if first_part is None else first_part + one
        second_part = two if second_part is None else second_part + two
    for a in range(3):
        for b in range(3):
            at = (a * 3 + b) * CH
            whole = sum_ref[0, a * CH : (a + 1) * CH, b * CH : (b + 1) * CH]
            whole = whole + first_part[:, (2 - a) * WIDE + b * CH : (2 - a) * WIDE + (b + 1) * CH]
            gw_ref[at : at + CH] = whole.astype(BF16)
            at = (TAPS + a * 3 + b) * CH
            whole = sum_ref[1, a * CH : (a + 1) * CH, b * CH : (b + 1) * CH]
            whole = whole + second_part[(2 - b) * WIDE + a * CH : (2 - b) * WIDE + (a + 1) * CH]
            gw_ref[at : at + CH] = whole.astype(BF16)


def forward_kernel(
    fwd_ref, use_ref, table_ref, first_ref, second_ref, above_ref, below_ref,
    out_ref,
    rows_ref, wide_ref, wide_act_ref, class_ref,
):
    class_ref[0:1] = above_ref[6 * CH :].astype(F32)[0:1]
    class_ref[9:10] = below_ref[6 * CH :].astype(F32)[0:1]
    for k in range(2):
        put_shifted(wide_ref, k, above_ref[(4 + k) * CH : (5 + k) * CH])
        put_shifted(wide_ref, 10 + k, below_ref[(4 + k) * CH : (5 + k) * CH])
    rows = jnp.swapaxes(fwd_ref[...], 0, 1)
    rows_ref[...] = rows
    for r in range(LOCAL):
        put_shifted(wide_ref, 2 + r, rows[r])
    class_ref[1:9] = use_ref[0].astype(F32) + 1.0
    terms = friction_terms(table_ref[...])

    def hidden_rows(step, carry):
        for k in range(5):
            r = 5 * step + k
            half = 0.5 * dot(first_ref[...], three_rows(wide_ref, r))
            act = (half + half * jnp.tanh(half)) * friction_row(terms, class_ref[pl.ds(r, 1)])
            put_shifted(wide_act_ref, r, act.astype(BF16))
        return carry

    lax.fori_loop(0, 2, hidden_rows, 0)

    def result_rows(step, carry):
        for k in range(4):
            r = 4 * step + k
            add = dot(second_ref[...], three_rows(wide_act_ref, r))
            out_ref[r] = (rows_ref[r].astype(F32) + add).astype(BF16)
        return carry

    lax.fori_loop(0, 2, result_rows, 0)


def grad_x_kernel(
    use_ref, grad_ref, first_ref, table_ref, inner_ref, outer_ref, near_ref, above_ref, flip2_ref,
    gx_ref,
    rows_ref, wide_ref, beside_ref, flip_ref,
):
    for i in range(2):
        for k in range(2):
            put_shifted(beside_ref.at[i], k, above_ref[(2 * i + k) * CH : (2 * i + k + 1) * CH])
            put_shifted(beside_ref.at[i], 2 + k, near_ref[i, k])
    for r in range(LOCAL - 2):
        put_shifted(wide_ref, 2 + r, inner_ref[r])
    for k in range(2):
        put_shifted(wide_ref, 8 + k, outer_ref[k])
    put_flipped(flip_ref, first_ref)
    terms = friction_terms(table_ref[...])
    for k, classes in enumerate((above_ref[6 * CH :].astype(F32)[1:2], use_ref[1, 0:1].astype(F32) + 1.0)):
        _, gh = backward_row(
            first_ref[...], flip2_ref[...], friction_row(terms, classes),
            three_rows(beside_ref.at[0], k), three_rows(beside_ref.at[1], k),
        )
        put_shifted(wide_ref, k, gh)
    rows_ref[...] = jnp.swapaxes(grad_ref[...], 0, 1)

    def result_rows(step, carry):
        for k in range(4):
            r = 4 * step + k
            add = dot(flip_ref[...], three_rows(wide_ref, r))
            gx_ref[r] = (rows_ref[r].astype(F32) + add).astype(BF16)
        return carry

    lax.fori_loop(0, 2, result_rows, 0)


def turn_kernel(act_ref, grad_ref, act_out_ref, grad_out_ref):
    act_out_ref[...] = jnp.swapaxes(act_ref[...], 0, 1)
    grad_out_ref[...] = jnp.swapaxes(grad_ref[...], 0, 1)


def sum_kernel(scale, parts_ref, out_ref):
    share = out_ref.shape[1] // 2
    total = jnp.sum(parts_ref[...].astype(F32), axis=0) * scale
    total = total[:share] + total[share:]
    both = jnp.concatenate([total, total], axis=0).astype(BF16)
    out_ref[...] = jnp.broadcast_to(both[None], out_ref.shape)


def spread_kernel(flat_ref, first_ref, second_ref):
    for a in range(3):
        for b in range(3):
            at = (a * 3 + b) * CH
            to = ((2 - a) * 3 + b) * CH
            first_ref[:, to : to + CH] = flat_ref[at : at + CH].astype(F32)
            at = (TAPS + a * 3 + b) * CH
            to = (b * 3 + 2 - a) * CH
            second_ref[:, to : to + CH] = flat_ref[at : at + CH].astype(F32)


def spread_out(values):
    count = lax.axis_size("rows")
    return lax.all_to_all(values.reshape(count, -1, 2, CH), "rows", 0, 0).reshape(values.shape)


def kernel_call(kernel, outs, scratch, name, flops, hbm, vmem, limit=24, smem=()):
    outs = [jax.ShapeDtypeStruct(dims, kind) for dims, kind in outs]
    scratch = [(x.shape, x.dtype) for x in hbm] + scratch
    sems = [pltpu.SemaphoreType.DMA((len(hbm),))] if hbm else []
    size = sum(x.size * x.dtype.itemsize for x in [*hbm, *vmem, *outs])
    spaces = [pltpu.SMEM] * len(smem) + [pltpu.HBM] * len(hbm) + [pltpu.VMEM] * len(vmem)
    return pl.pallas_call(
        kernel,
        in_specs=[pl.BlockSpec(memory_space=space) for space in spaces],
        out_shape=outs,
        scratch_shapes=[pltpu.VMEM(dims, kind) for dims, kind in scratch] + sems,
        cost_estimate=pl.CostEstimate(flops=flops, bytes_accessed=size, transcendentals=0),
        compiler_params=pltpu.CompilerParams(vmem_limit_bytes=limit * 1024 * 1024),
        name=name,
    )(*smem, *hbm, *vmem)


def body(fwd_in, bwd_in, grad_in, land_use, friction, weight_in, weight_out):
    row_count = lax.axis_size("rows")
    sections = lax.axis_size("pipe")
    fwd, bwd, grad = fwd_in[0], bwd_in[0], grad_in[0]
    use, table, first, second = land_use[0], friction[0].T, weight_in[0], weight_out[0]
    scale = 1.0 / (LOCAL * row_count * COLS) ** 0.5
    share = 2 * TAPS * CH // row_count
    cells, weight = (CH, LOCAL, COLS), (CH, TAPS * CH)
    row, wide = (CH, COLS), (WIDE, COLS)
    row_flops = 2 * CH * TAPS * CH * COLS
    down = [(i, i + 1) for i in range(row_count - 1)]
    up = [(i + 1, i) for i in range(row_count - 1)]

    head, tail = kernel_call(
        edges_kernel, [((6 * CH + 16, COLS), BF16)] * 2, [], "edges", 0, [bwd, grad, fwd, use], [], 56
    )
    below, above = lax.ppermute(head, "rows", up), lax.ppermute(tail, "rows", down)
    top = (lax.axis_index("rows") == 0).astype(F32).reshape(1)
    gh_inner, near, sums, fric, flip = kernel_call(
        inner_kernel,
        [((LOCAL - 2, *row), BF16), ((2, 4, *row), BF16), ((2, WIDE, WIDE), F32), (row, F32), (weight, BF16)],
        [((LOCAL + 1, *wide), BF16)] * 2 + [((10, *row), BF16)] * 2 + [((LOCAL, COLS), F32)],
        "inner", 30 * row_flops,
        [], [bwd, grad, use, table, first, second], smem=[top],
    )
    gh_outer, partial = kernel_call(
        outer_kernel,
        [((2, *row), BF16), ((row_count * share, CH), BF16)],
        [((2, 4, *wide), BF16)],
        "outer", 8 * row_flops,
        [], [table, first, near, below, fric, flip, sums],
    )
    partial, above = lax.optimization_barrier((partial, above))
    shares = spread_out(partial)

    fwd, gh_outer = lax.optimization_barrier((fwd, gh_outer))
    (result,) = kernel_call(
        forward_kernel,
        [((LOCAL, *row), BF16)],
        [((LOCAL, *row), BF16), ((12, *wide), BF16), ((10, *wide), BF16), ((16, COLS), F32)],
        "forward", 18 * row_flops,
        [], [fwd, use, table, first, second, above, below],
    )
    handed_act = lax.ppermute(result, "pipe", [(i, i + 1) for i in range(sections - 1)])
    (grad_x,) = kernel_call(
        grad_x_kernel,
        [((LOCAL, *row), BF16)],
        [((LOCAL, *row), BF16), ((10, *wide), BF16), ((2, 4, *wide), BF16), (weight, BF16)],
        "grad_x", 12 * row_flops,
        [], [use, grad, first, table, gh_inner, gh_outer, near, above, flip],
    )
    handed_grad = lax.ppermute(grad_x, "pipe", [(i + 1, i) for i in range(sections - 1)])
    handed_act, handed_grad = kernel_call(
        turn_kernel, [(cells, BF16)] * 2, [], "turn", 0, [], [handed_act, handed_grad]
    )
    shares, result, grad_x = lax.optimization_barrier((shares, result, grad_x))

    pairs = (row_count // 2, 2 * share, CH)
    (summed,) = kernel_call(
        lambda *refs: sum_kernel(scale, *refs), [(pairs, BF16)], [], "sum_shares", 0, [], [shares.reshape(pairs)]
    )
    gathered = spread_out(summed.reshape(partial.shape))
    grad_first, grad_second = kernel_call(spread_kernel, [(weight, F32)] * 2, [], "spread", 0, [], [gathered])
    return (handed_act[None], handed_grad[None], grad_first[None], grad_second[None])


def solution(mesh):
    cells = P("pipe", None, "rows", None)
    own = P("pipe", None, None)
    return jax.shard_map(
        body,
        mesh=mesh,
        in_specs=(cells, cells, cells, cells, own, own, own),
        out_specs=(cells, cells, own, own),
        check_vma=False,
    )
```

```python
import jax
import jax.numpy as jnp
from jax import lax
from jax.experimental import pallas as pl
from jax.experimental.pallas import tpu as pltpu
from jax.sharding import PartitionSpec as P

CH = 128
COLS = 256
LOCAL = 8
CLASSES = 8
TAPS = 9
WIDE = 3 * CH
BF16 = jnp.bfloat16
F32 = jnp.float32


def fetch(sems, *pairs):
    copies = [pltpu.make_async_copy(src, dst, sems.at[i]) for i, (src, dst) in enumerate(pairs)]
    for copy in copies:
        copy.start()
    return copies


def edges_kernel(bwd_hbm, grad_hbm, fwd_hbm, use_hbm, head_ref, tail_ref, bwd_ref, grad_ref, fwd_ref, use_ref, sems):
    copies = fetch(sems, (bwd_hbm, bwd_ref), (grad_hbm, grad_ref), (fwd_hbm, fwd_ref), (use_hbm, use_ref))
    for i, ref in enumerate((bwd_ref, grad_ref, fwd_ref)):
        copies[i].wait()
        rows = jnp.swapaxes(ref[...], 0, 1)
        for k in range(2):
            head_ref[(2 * i + k) * CH : (2 * i + k + 1) * CH] = rows[k]
            tail_ref[(2 * i + k) * CH : (2 * i + k + 1) * CH] = rows[LOCAL - 2 + k]
    copies[3].wait()
    sub = lax.broadcasted_iota(jnp.int32, (16, COLS), 0)
    for out, edge in ((head_ref, 0), (tail_ref, LOCAL - 1)):
        ahead = use_ref[0, edge : edge + 1, :].astype(F32) + 1.0
        back = use_ref[1, edge : edge + 1, :].astype(F32) + 1.0
        out[6 * CH :] = jnp.where(sub == 0, ahead, jnp.where(sub == 1, back, 0.0)).astype(BF16)


def put_shifted(wide_ref, at, row):
    lane = lax.broadcasted_iota(jnp.int32, (CH, COLS), 1)
    zero = jnp.zeros((CH, COLS), BF16)
    wide_ref[at, 0:CH] = jnp.where(lane == 0, zero, pltpu.roll(row, 1, 1))
    wide_ref[at, CH : 2 * CH] = row
    wide_ref[at, 2 * CH :] = jnp.where(lane == COLS - 1, zero, pltpu.roll(row, COLS - 1, 1))


def three_rows(ref, at):
    return ref[pl.ds(at, 3)].reshape(-1, COLS)


def dot(a, b):
    return jnp.dot(a, b, preferred_element_type=F32)


def dot_cells(a, b):
    return lax.dot_general(a, b, (((1,), (1,)), ((), ())), preferred_element_type=F32)


def put_flipped(flip_ref, weight_ref):
    for t in range(TAPS):
        mirrored = (TAPS - 1 - t) * CH
        flip_ref[:, mirrored : mirrored + CH] = weight_ref[:, t * CH : (t + 1) * CH].T


def friction_terms(table):
    high = table.astype(BF16).astype(F32)
    middle = (table - high).astype(BF16).astype(F32)
    low = table - high - middle
    return jnp.concatenate([high, middle, low], axis=0).T.astype(BF16)


def friction_row(terms, classes):
    level = (lax.broadcasted_iota(jnp.int32, (3 * CLASSES, COLS), 0) % CLASSES + 1).astype(F32)
    return dot(terms, jnp.where(classes == level, 1.0, 0.0).astype(BF16))


def backward_row(first, flip2, fric, stored_rows, grad_rows):
    hb = dot(first, stored_rows)
    sig = 0.5 + 0.5 * jnp.tanh(0.5 * hb)
    active = (hb * sig * fric).astype(BF16)
    ga = dot(flip2, grad_rows)
    return active, (ga * fric * (sig * (1.0 + hb * (1.0 - sig)))).astype(BF16)


def inner_kernel(
    top_ref, bwd_ref, grad_ref, use_ref, table_ref, first_ref, second_ref,
    gh_out_ref, near_ref, sum_ref, fric_ref, flip_ref,
    wide_b_ref, wide_g_ref, actb_ref, gh_ref, class_ref,
):
    for ref in (actb_ref, gh_ref):
        for r in (0, 8, 9):
            ref[r] = jnp.zeros((CH, COLS), BF16)
    put_flipped(flip_ref, second_ref)
    for i, (ref, wide_ref) in enumerate(((bwd_ref, wide_b_ref), (grad_ref, wide_g_ref))):
        rows = jnp.swapaxes(ref[...], 0, 1)
        wide_ref[0] = jnp.zeros((WIDE, COLS), BF16)
        for r in range(LOCAL):
            put_shifted(wide_ref, r + 1, rows[r])
        for k, r in enumerate((0, 1, LOCAL - 2, LOCAL - 1)):
            near_ref[i, k] = rows[r]
    class_ref[...] = use_ref[1].astype(F32) + 1.0
    terms = friction_terms(table_ref[...])
    fric_ref[...] = friction_row(terms, class_ref[LOCAL - 1 : LOCAL])
    active, gh = backward_row(
        first_ref[...], flip_ref[...], friction_row(terms, class_ref[0:1] * top_ref[0]),
        three_rows(wide_b_ref, 0), three_rows(wide_g_ref, 0),
    )
    actb_ref[1] = active
    gh_ref[1] = gh

    def step(n, carry):
        for k in range(3):
            r = 3 * n + k + 1
            active, gh = backward_row(
                first_ref[...], flip_ref[...], friction_row(terms, class_ref[pl.ds(r, 1)]),
                three_rows(wide_b_ref, r), three_rows(wide_g_ref, r),
            )
            actb_ref[r + 1] = active
            gh_ref[r + 1] = gh
            gh_out_ref[r - 1] = gh
        return carry

    lax.fori_loop(0, 2, step, 0)
    total = None
    for r in range(LOCAL):
        part = dot_cells(three_rows(gh_ref, r), wide_b_ref[r + 1])
        total = part if total is None else total + part
    sum_ref[0] = total
    total = None
    for r in range(LOCAL):
        part = dot_cells(wide_g_ref[r + 1], three_rows(actb_ref, r))
        total = part if total is None else total + part
    sum_ref[1] = total


def outer_kernel(
    table_ref, first_ref, near_ref, below_ref, fric_ref, flip_ref, sum_ref,
    gh_out_ref, gw_hbm,
    wide_ref, gw_ref, sems,
):
    for i in range(2):
        for k in range(2):
            put_shifted(wide_ref.at[i], k, near_ref[i, 2 + k])
            put_shifted(wide_ref.at[i], 2 + k, below_ref[(2 * i + k) * CH : (2 * i + k + 1) * CH])
    last = friction_row(friction_terms(table_ref[...]), below_ref[6 * CH :].astype(F32)[1:2])
    rows = []
    for k, fric in enumerate((fric_ref[...], last)):
        stored_rows, grad_rows = three_rows(wide_ref.at[0], k), three_rows(wide_ref.at[1], k)
        active, gh = backward_row(first_ref[...], flip_ref[...], fric, stored_rows, grad_rows)
        gh_out_ref[k] = gh
        rows.append((stored_rows, grad_rows, active, gh))
    half = TAPS * CH

    def send(n):
        part = pl.ds(n * half, half)
        copy = pltpu.make_async_copy(gw_ref.at[part], gw_hbm.at[part], sems.at[n])
        copy.start()
        return copy

    part = sum(dot_cells(gh, stored_rows) for stored_rows, _, _, gh in rows)
    for a in range(3):
        for b in range(3):
            at = (a * 3 + b) * CH
            whole = sum_ref[0, a * CH : (a + 1) * CH, b * CH : (b + 1) * CH]
            whole = whole + part[:, (2 - a) * WIDE + b * CH : (2 - a) * WIDE + (b + 1) * CH]
            gw_ref[at : at + CH] = whole.astype(BF16)
    sent_first = send(0)
    part = sum(dot_cells(grad_rows, active) for _, grad_rows, active, _ in rows)
    for a in range(3):
        for b in range(3):
            at = (TAPS + a * 3 + b) * CH
            whole = sum_ref[1, a * CH : (a + 1) * CH, b * CH : (b + 1) * CH]
            whole = whole + part[(2 - b) * WIDE + a * CH : (2 - b) * WIDE + (a + 1) * CH]
            gw_ref[at : at + CH] = whole.astype(BF16)
    sent_second = send(1)
    sent_first.wait()
    sent_second.wait()


def forward_kernel(
    fwd_ref, use_ref, table_ref, first_ref, second_ref, above_ref, below_ref,
    out_ref,
    rows_ref, wide_ref, wide_act_ref, class_ref,
):
    class_ref[0:1] = above_ref[6 * CH :].astype(F32)[0:1]
    class_ref[9:10] = below_ref[6 * CH :].astype(F32)[0:1]
    for k in range(2):
        put_shifted(wide_ref, k, above_ref[(4 + k) * CH : (5 + k) * CH])
        put_shifted(wide_ref, 10 + k, below_ref[(4 + k) * CH : (5 + k) * CH])
    rows = jnp.swapaxes(fwd_ref[...], 0, 1)
    rows_ref[...] = rows
    for r in range(LOCAL):
        put_shifted(wide_ref, 2 + r, rows[r])
    class_ref[1:9] = use_ref[0].astype(F32) + 1.0
    terms = friction_terms(table_ref[...])

    def hidden_rows(step, carry):
        for k in range(5):
            r = 5 * step + k
            half = 0.5 * dot(first_ref[...], three_rows(wide_ref, r))
            act = (half + half * jnp.tanh(half)) * friction_row(terms, class_ref[pl.ds(r, 1)])
            put_shifted(wide_act_ref, r, act.astype(BF16))
        return carry

    lax.fori_loop(0, 2, hidden_rows, 0)

    def result_rows(step, carry):
        for k in range(4):
            r = 4 * step + k
            add = dot(second_ref[...], three_rows(wide_act_ref, r))
            out_ref[r] = (rows_ref[r].astype(F32) + add).astype(BF16)
        return carry

    lax.fori_loop(0, 2, result_rows, 0)


def grad_x_kernel(
    use_ref, grad_ref, first_ref, table_ref, inner_ref, outer_ref, near_ref, above_ref, flip2_ref,
    gx_ref,
    rows_ref, wide_ref, beside_ref, flip_ref,
):
    for i in range(2):
        for k in range(2):
            put_shifted(beside_ref.at[i], k, above_ref[(2 * i + k) * CH : (2 * i + k + 1) * CH])
            put_shifted(beside_ref.at[i], 2 + k, near_ref[i, k])
    for r in range(LOCAL - 2):
        put_shifted(wide_ref, 2 + r, inner_ref[r])
    for k in range(2):
        put_shifted(wide_ref, 8 + k, outer_ref[k])
    put_flipped(flip_ref, first_ref)
    terms = friction_terms(table_ref[...])
    for k, classes in enumerate((above_ref[6 * CH :].astype(F32)[1:2], use_ref[1, 0:1].astype(F32) + 1.0)):
        _, gh = backward_row(
            first_ref[...], flip2_ref[...], friction_row(terms, classes),
            three_rows(beside_ref.at[0], k), three_rows(beside_ref.at[1], k),
        )
        put_shifted(wide_ref, k, gh)
    rows_ref[...] = jnp.swapaxes(grad_ref[...], 0, 1)

    def result_rows(step, carry):
        for k in range(4):
            r = 4 * step + k
            add = dot(flip_ref[...], three_rows(wide_ref, r))
            gx_ref[r] = (rows_ref[r].astype(F32) + add).astype(BF16)
        return carry

    lax.fori_loop(0, 2, result_rows, 0)


def turn_kernel(act_ref, grad_ref, act_out_ref, grad_out_ref):
    act_out_ref[...] = jnp.swapaxes(act_ref[...], 0, 1)
    grad_out_ref[...] = jnp.swapaxes(grad_ref[...], 0, 1)


def sum_kernel(scale, parts_ref, out_ref):
    share = out_ref.shape[1] // 2
    total = jnp.sum(parts_ref[...].astype(F32), axis=0) * scale
    total = total[:share] + total[share:]
    both = jnp.concatenate([total, total], axis=0).astype(BF16)
    out_ref[...] = jnp.broadcast_to(both[None], out_ref.shape)


def spread_kernel(flat_ref, first_ref, second_ref):
    for a in range(3):
        for b in range(3):
            at = (a * 3 + b) * CH
            to = ((2 - a) * 3 + b) * CH
            first_ref[:, to : to + CH] = flat_ref[at : at + CH].astype(F32)
            at = (TAPS + a * 3 + b) * CH
            to = (b * 3 + 2 - a) * CH
            second_ref[:, to : to + CH] = flat_ref[at : at + CH].astype(F32)


def spread_out(values):
    count = lax.axis_size("rows")
    return lax.all_to_all(values.reshape(count, -1, 2, CH), "rows", 0, 0).reshape(values.shape)


def kernel_call(kernel, outs, scratch, name, flops, hbm, vmem, limit=24, smem=(), out_sems=0):
    out_places = [pltpu.HBM if isinstance(kind, list) else pltpu.VMEM for _, kind in outs]
    outs = [jax.ShapeDtypeStruct(dims, kind[0] if isinstance(kind, list) else kind) for dims, kind in outs]
    scratch = [(x.shape, x.dtype) for x in hbm] + scratch
    sems = [pltpu.SemaphoreType.DMA((count,)) for count in (out_sems, len(hbm)) if count]
    size = sum(x.size * x.dtype.itemsize for x in [*hbm, *vmem, *outs])
    spaces = [pltpu.SMEM] * len(smem) + [pltpu.HBM] * len(hbm) + [pltpu.VMEM] * len(vmem)
    return pl.pallas_call(
        kernel,
        in_specs=[pl.BlockSpec(memory_space=space) for space in spaces],
        out_specs=[pl.BlockSpec(memory_space=place) for place in out_places],
        out_shape=outs,
        scratch_shapes=[pltpu.VMEM(dims, kind) for dims, kind in scratch] + sems,
        cost_estimate=pl.CostEstimate(flops=flops, bytes_accessed=size, transcendentals=0),
        compiler_params=pltpu.CompilerParams(vmem_limit_bytes=limit * 1024 * 1024),
        name=name,
    )(*smem, *hbm, *vmem)


def body(fwd_in, bwd_in, grad_in, land_use, friction, weight_in, weight_out):
    row_count = lax.axis_size("rows")
    sections = lax.axis_size("pipe")
    fwd, bwd, grad = fwd_in[0], bwd_in[0], grad_in[0]
    use, table, first, second = land_use[0], friction[0].T, weight_in[0], weight_out[0]
    scale = 1.0 / (LOCAL * row_count * COLS) ** 0.5
    share = 2 * TAPS * CH // row_count
    cells, weight = (CH, LOCAL, COLS), (CH, TAPS * CH)
    row, wide = (CH, COLS), (WIDE, COLS)
    row_flops = 2 * CH * TAPS * CH * COLS
    down = [(i, i + 1) for i in range(row_count - 1)]
    up = [(i + 1, i) for i in range(row_count - 1)]

    head, tail = kernel_call(
        edges_kernel, [((6 * CH + 16, COLS), BF16)] * 2, [], "edges", 0, [bwd, grad, fwd, use], [], 56
    )
    below, above = lax.ppermute(head, "rows", up), lax.ppermute(tail, "rows", down)
    top = (lax.axis_index("rows") == 0).astype(F32).reshape(1)
    gh_inner, near, sums, fric, flip = kernel_call(
        inner_kernel,
        [((LOCAL - 2, *row), BF16), ((2, 4, *row), BF16), ((2, WIDE, WIDE), F32), (row, F32), (weight, BF16)],
        [((LOCAL + 1, *wide), BF16)] * 2 + [((10, *row), BF16)] * 2 + [((LOCAL, COLS), F32)],
        "inner", 30 * row_flops,
        [], [bwd, grad, use, table, first, second], smem=[top],
    )
    gh_outer, partial = kernel_call(
        outer_kernel,
        [((2, *row), BF16), ((2 * TAPS * CH, CH), [BF16])],
        [((2, 4, *wide), BF16), ((2 * TAPS * CH, CH), BF16)],
        "outer", 8 * row_flops,
        [], [table, first, near, below, fric, flip, sums], out_sems=2,
    )
    partial, above = lax.optimization_barrier((partial, above))
    shares = spread_out(partial)

    fwd, gh_outer = lax.optimization_barrier((fwd, gh_outer))
    (result,) = kernel_call(
        forward_kernel,
        [((LOCAL, *row), BF16)],
        [((LOCAL, *row), BF16), ((12, *wide), BF16), ((10, *wide), BF16), ((16, COLS), F32)],
        "forward", 18 * row_flops,
        [], [fwd, use, table, first, second, above, below],
    )
    handed_act = lax.ppermute(result, "pipe", [(i, i + 1) for i in range(sections - 1)])
    (grad_x,) = kernel_call(
        grad_x_kernel,
        [((LOCAL, *row), BF16)],
        [((LOCAL, *row), BF16), ((10, *wide), BF16), ((2, 4, *wide), BF16), (weight, BF16)],
        "grad_x", 12 * row_flops,
        [], [use, grad, first, table, gh_inner, gh_outer, near, above, flip],
    )
    handed_grad = lax.ppermute(grad_x, "pipe", [(i + 1, i) for i in range(sections - 1)])
    handed_act, handed_grad = kernel_call(
        turn_kernel, [(cells, BF16)] * 2, [], "turn", 0, [], [handed_act, handed_grad]
    )
    shares, result, grad_x = lax.optimization_barrier((shares, result, grad_x))

    pairs = (row_count // 2, 2 * share, CH)
    (summed,) = kernel_call(
        lambda *refs: sum_kernel(scale, *refs), [(pairs, BF16)], [], "sum_shares", 0, [], [shares.reshape(pairs)]
    )
    gathered = spread_out(summed.reshape(partial.shape))
    grad_first, grad_second = kernel_call(spread_kernel, [(weight, F32)] * 2, [], "spread", 0, [], [gathered])
    return (handed_act[None], handed_grad[None], grad_first[None], grad_second[None])


def solution(mesh):
    cells = P("pipe", None, "rows", None)
    own = P("pipe", None, None)
    return jax.shard_map(
        body,
        mesh=mesh,
        in_specs=(cells, cells, cells, cells, own, own, own),
        out_specs=(cells, cells, own, own),
        check_vma=False,
    )
```

```python
import jax
import jax.numpy as jnp
from jax import lax
from jax.experimental import pallas as pl
from jax.experimental.pallas import tpu as pltpu
from jax.sharding import PartitionSpec as P

CH = 128
COLS = 256
LOCAL = 8
CLASSES = 8
TAPS = 9
WIDE = 3 * CH
BF16 = jnp.bfloat16
F32 = jnp.float32


def fetch(sems, *pairs):
    copies = [pltpu.make_async_copy(src, dst, sems.at[i]) for i, (src, dst) in enumerate(pairs)]
    for copy in copies:
        copy.start()
    return copies


def edges_kernel(bwd_hbm, grad_hbm, fwd_hbm, use_hbm, head_ref, tail_ref, bwd_ref, grad_ref, fwd_ref, use_ref, sems):
    copies = fetch(sems, (bwd_hbm, bwd_ref), (grad_hbm, grad_ref), (fwd_hbm, fwd_ref), (use_hbm, use_ref))
    for i, ref in enumerate((bwd_ref, grad_ref, fwd_ref)):
        copies[i].wait()
        rows = jnp.swapaxes(ref[...], 0, 1)
        for k in range(2):
            head_ref[(2 * i + k) * CH : (2 * i + k + 1) * CH] = rows[k]
            tail_ref[(2 * i + k) * CH : (2 * i + k + 1) * CH] = rows[LOCAL - 2 + k]
    copies[3].wait()
    sub = lax.broadcasted_iota(jnp.int32, (16, COLS), 0)
    for out, edge in ((head_ref, 0), (tail_ref, LOCAL - 1)):
        ahead = use_ref[0, edge : edge + 1, :].astype(F32) + 1.0
        back = use_ref[1, edge : edge + 1, :].astype(F32) + 1.0
        out[6 * CH :] = jnp.where(sub == 0, ahead, jnp.where(sub == 1, back, 0.0)).astype(BF16)


def put_shifted(wide_ref, at, row):
    lane = lax.broadcasted_iota(jnp.int32, (CH, COLS), 1)
    zero = jnp.zeros((CH, COLS), BF16)
    wide_ref[at, 0:CH] = jnp.where(lane == 0, zero, pltpu.roll(row, 1, 1))
    wide_ref[at, CH : 2 * CH] = row
    wide_ref[at, 2 * CH :] = jnp.where(lane == COLS - 1, zero, pltpu.roll(row, COLS - 1, 1))


def three_rows(ref, at):
    return ref[pl.ds(at, 3)].reshape(-1, COLS)


def dot(a, b):
    return jnp.dot(a, b, preferred_element_type=F32)


def dot_cells(a, b):
    return lax.dot_general(a, b, (((1,), (1,)), ((), ())), preferred_element_type=F32)


def put_flipped(flip_ref, weight_ref):
    for t in range(TAPS):
        mirrored = (TAPS - 1 - t) * CH
        flip_ref[:, mirrored : mirrored + CH] = weight_ref[:, t * CH : (t + 1) * CH].T


def friction_terms(table):
    high = table.astype(BF16).astype(F32)
    middle = (table - high).astype(BF16).astype(F32)
    low = table - high - middle
    return jnp.concatenate([high, middle, low], axis=0).T.astype(BF16)


def friction_row(terms, classes):
    level = (lax.broadcasted_iota(jnp.int32, (3 * CLASSES, COLS), 0) % CLASSES + 1).astype(F32)
    return dot(terms, jnp.where(classes == level, 1.0, 0.0).astype(BF16))


def backward_row(first, flip2, fric, stored_rows, grad_rows):
    hb = dot(first, stored_rows)
    sig = 0.5 + 0.5 * jnp.tanh(0.5 * hb)
    active = (hb * sig * fric).astype(BF16)
    ga = dot(flip2, grad_rows)
    return active, (ga * fric * (sig * (1.0 + hb * (1.0 - sig)))).astype(BF16)


def inner_kernel(
    top_ref, bwd_ref, grad_ref, use_ref, table_ref, first_ref, second_ref,
    gh_out_ref, near_ref, sum_ref, fric_ref, flip_ref,
    wide_b_ref, wide_g_ref, actb_ref, gh_ref, class_ref,
):
    for ref in (actb_ref, gh_ref):
        for r in (0, 8, 9):
            ref[r] = jnp.zeros((CH, COLS), BF16)
    put_flipped(flip_ref, second_ref)
    for i, (ref, wide_ref) in enumerate(((bwd_ref, wide_b_ref), (grad_ref, wide_g_ref))):
        rows = jnp.swapaxes(ref[...], 0, 1)
        wide_ref[0] = jnp.zeros((WIDE, COLS), BF16)
        for r in range(LOCAL):
            put_shifted(wide_ref, r + 1, rows[r])
        for k, r in enumerate((0, 1, LOCAL - 2, LOCAL - 1)):
            near_ref[i, k] = rows[r]
    class_ref[...] = use_ref[1].astype(F32) + 1.0
    terms = friction_terms(table_ref[...])
    fric_ref[...] = friction_row(terms, class_ref[LOCAL - 1 : LOCAL])
    active, gh = backward_row(
        first_ref[...], flip_ref[...], friction_row(terms, class_ref[0:1] * top_ref[0]),
        three_rows(wide_b_ref, 0), three_rows(wide_g_ref, 0),
    )
    actb_ref[1] = active
    gh_ref[1] = gh

    def step(n, carry):
        for k in range(3):
            r = 3 * n + k + 1
            active, gh = backward_row(
                first_ref[...], flip_ref[...], friction_row(terms, class_ref[pl.ds(r, 1)]),
                three_rows(wide_b_ref, r), three_rows(wide_g_ref, r),
            )
            actb_ref[r + 1] = active
            gh_ref[r + 1] = gh
            gh_out_ref[r - 1] = gh
        return carry

    lax.fori_loop(0, 2, step, 0)
    total = None
    for r in range(LOCAL):
        part = dot_cells(three_rows(gh_ref, r), wide_b_ref[r + 1])
        total = part if total is None else total + part
    sum_ref[0] = total
    total = None
    for r in range(LOCAL):
        part = dot_cells(wide_g_ref[r + 1], three_rows(actb_ref, r))
        total = part if total is None else total + part
    sum_ref[1] = total


def outer_kernel(
    table_ref, first_ref, near_ref, below_ref, fric_ref, flip_ref, sum_ref,
    gh_out_ref, gw_ref,
    wide_ref,
):
    for i in range(2):
        for k in range(2):
            put_shifted(wide_ref.at[i], k, near_ref[i, 2 + k])
            put_shifted(wide_ref.at[i], 2 + k, below_ref[(2 * i + k) * CH : (2 * i + k + 1) * CH])
    last = friction_row(friction_terms(table_ref[...]), below_ref[6 * CH :].astype(F32)[1:2])
    first_part = second_part = None
    for k, fric in enumerate((fric_ref[...], last)):
        stored_rows, grad_rows = three_rows(wide_ref.at[0], k), three_rows(wide_ref.at[1], k)
        active, gh = backward_row(first_ref[...], flip_ref[...], fric, stored_rows, grad_rows)
        gh_out_ref[k] = gh
        one, two = dot_cells(gh, stored_rows), dot_cells(grad_rows, active)
        first_part = one if first_part is None else first_part + one
        second_part = two if second_part is None else second_part + two
    for a in range(3):
        for b in range(3):
            at = (a * 3 + b) * CH
            whole = sum_ref[0, a * CH : (a + 1) * CH, b * CH : (b + 1) * CH]
            whole = whole + first_part[:, (2 - a) * WIDE + b * CH : (2 - a) * WIDE + (b + 1) * CH]
            gw_ref[at : at + CH] = whole.astype(BF16)
            at = (TAPS + a * 3 + b) * CH
            whole = sum_ref[1, a * CH : (a + 1) * CH, b * CH : (b + 1) * CH]
            whole = whole + second_part[(2 - b) * WIDE + a * CH : (2 - b) * WIDE + (a + 1) * CH]
            gw_ref[at : at + CH] = whole.astype(BF16)


def forward_kernel(
    fwd_ref, use_ref, table_ref, first_ref, second_ref, above_ref, below_ref,
    out_ref,
    rows_ref, wide_ref, wide_act_ref, class_ref,
):
    class_ref[0:1] = above_ref[6 * CH :].astype(F32)[0:1]
    class_ref[9:10] = below_ref[6 * CH :].astype(F32)[0:1]
    for k in range(2):
        put_shifted(wide_ref, k, above_ref[(4 + k) * CH : (5 + k) * CH])
        put_shifted(wide_ref, 10 + k, below_ref[(4 + k) * CH : (5 + k) * CH])
    rows = jnp.swapaxes(fwd_ref[...], 0, 1)
    rows_ref[...] = rows
    for r in range(LOCAL):
        put_shifted(wide_ref, 2 + r, rows[r])
    class_ref[1:9] = use_ref[0].astype(F32) + 1.0
    terms = friction_terms(table_ref[...])

    def hidden_rows(step, carry):
        for k in range(5):
            r = 5 * step + k
            half = 0.5 * dot(first_ref[...], three_rows(wide_ref, r))
            act = (half + half * jnp.tanh(half)) * friction_row(terms, class_ref[pl.ds(r, 1)])
            put_shifted(wide_act_ref, r, act.astype(BF16))
        return carry

    lax.fori_loop(0, 2, hidden_rows, 0)

    def result_rows(step, carry):
        for k in range(4):
            r = 4 * step + k
            add = dot(second_ref[...], three_rows(wide_act_ref, r))
            out_ref[r] = (rows_ref[r].astype(F32) + add).astype(BF16)
        return carry

    lax.fori_loop(0, 2, result_rows, 0)


def grad_x_kernel(
    use_ref, grad_ref, first_ref, table_ref, inner_ref, outer_ref, near_ref, above_ref, flip2_ref,
    gx_ref,
    rows_ref, wide_ref, beside_ref, flip_ref,
):
    for i in range(2):
        for k in range(2):
            put_shifted(beside_ref.at[i], k, above_ref[(2 * i + k) * CH : (2 * i + k + 1) * CH])
            put_shifted(beside_ref.at[i], 2 + k, near_ref[i, k])
    for r in range(LOCAL - 2):
        put_shifted(wide_ref, 2 + r, inner_ref[r])
    for k in range(2):
        put_shifted(wide_ref, 8 + k, outer_ref[k])
    put_flipped(flip_ref, first_ref)
    terms = friction_terms(table_ref[...])
    for k, classes in enumerate((above_ref[6 * CH :].astype(F32)[1:2], use_ref[1, 0:1].astype(F32) + 1.0)):
        _, gh = backward_row(
            first_ref[...], flip2_ref[...], friction_row(terms, classes),
            three_rows(beside_ref.at[0], k), three_rows(beside_ref.at[1], k),
        )
        put_shifted(wide_ref, k, gh)
    rows_ref[...] = jnp.swapaxes(grad_ref[...], 0, 1)

    def result_rows(step, carry):
        for k in range(4):
            r = 4 * step + k
            add = dot(flip_ref[...], three_rows(wide_ref, r))
            gx_ref[r] = (rows_ref[r].astype(F32) + add).astype(BF16)
        return carry

    lax.fori_loop(0, 2, result_rows, 0)


def turn_kernel(act_ref, grad_ref, act_out_ref, grad_out_ref):
    act_out_ref[...] = jnp.swapaxes(act_ref[...], 0, 1)
    grad_out_ref[...] = jnp.swapaxes(grad_ref[...], 0, 1)


def sum_kernel(scale, parts_ref, out_ref):
    share = out_ref.shape[1] // 2
    total = jnp.sum(parts_ref[...].astype(F32), axis=0) * scale
    total = total[:share] + total[share:]
    both = jnp.concatenate([total, total], axis=0).astype(BF16)
    out_ref[...] = jnp.broadcast_to(both[None], out_ref.shape)


def spread_kernel(flat_ref, first_ref, second_ref):
    for a in range(3):
        for b in range(3):
            at = (a * 3 + b) * CH
            to = ((2 - a) * 3 + b) * CH
            first_ref[:, to : to + CH] = flat_ref[at : at + CH].astype(F32)
            at = (TAPS + a * 3 + b) * CH
            to = (b * 3 + 2 - a) * CH
            second_ref[:, to : to + CH] = flat_ref[at : at + CH].astype(F32)


def section_rows(sections, row_count):
    groups = []
    for section in range(sections):
        line = [(k * 27 if section % 2 else k * 37) % row_count for k in range(row_count)]
        groups.append([section * row_count + k for k in line])
    return groups


def spread_out(values):
    count = lax.axis_size("rows")
    groups = section_rows(lax.axis_size("pipe"), count)
    parts = lax.all_to_all(values.reshape(count, -1, 2, CH), ("pipe", "rows"), 0, 0, axis_index_groups=groups)
    return parts.reshape(values.shape)


def kernel_call(kernel, outs, scratch, name, flops, hbm, vmem, limit=24, smem=()):
    outs = [jax.ShapeDtypeStruct(dims, kind) for dims, kind in outs]
    scratch = [(x.shape, x.dtype) for x in hbm] + scratch
    sems = [pltpu.SemaphoreType.DMA((len(hbm),))] if hbm else []
    size = sum(x.size * x.dtype.itemsize for x in [*hbm, *vmem, *outs])
    spaces = [pltpu.SMEM] * len(smem) + [pltpu.HBM] * len(hbm) + [pltpu.VMEM] * len(vmem)
    return pl.pallas_call(
        kernel,
        in_specs=[pl.BlockSpec(memory_space=space) for space in spaces],
        out_shape=outs,
        scratch_shapes=[pltpu.VMEM(dims, kind) for dims, kind in scratch] + sems,
        cost_estimate=pl.CostEstimate(flops=flops, bytes_accessed=size, transcendentals=0),
        compiler_params=pltpu.CompilerParams(vmem_limit_bytes=limit * 1024 * 1024),
        name=name,
    )(*smem, *hbm, *vmem)


def body(fwd_in, bwd_in, grad_in, land_use, friction, weight_in, weight_out):
    row_count = lax.axis_size("rows")
    sections = lax.axis_size("pipe")
    fwd, bwd, grad = fwd_in[0], bwd_in[0], grad_in[0]
    use, table, first, second = land_use[0], friction[0].T, weight_in[0], weight_out[0]
    scale = 1.0 / (LOCAL * row_count * COLS) ** 0.5
    share = 2 * TAPS * CH // row_count
    cells, weight = (CH, LOCAL, COLS), (CH, TAPS * CH)
    row, wide = (CH, COLS), (WIDE, COLS)
    row_flops = 2 * CH * TAPS * CH * COLS
    down = [(i, i + 1) for i in range(row_count - 1)]
    up = [(i + 1, i) for i in range(row_count - 1)]

    head, tail = kernel_call(
        edges_kernel, [((6 * CH + 16, COLS), BF16)] * 2, [], "edges", 0, [bwd, grad, fwd, use], [], 56
    )
    below, above = lax.ppermute(head, "rows", up), lax.ppermute(tail, "rows", down)
    top = (lax.axis_index("rows") == 0).astype(F32).reshape(1)
    gh_inner, near, sums, fric, flip = kernel_call(
        inner_kernel,
        [((LOCAL - 2, *row), BF16), ((2, 4, *row), BF16), ((2, WIDE, WIDE), F32), (row, F32), (weight, BF16)],
        [((LOCAL + 1, *wide), BF16)] * 2 + [((10, *row), BF16)] * 2 + [((LOCAL, COLS), F32)],
        "inner", 30 * row_flops,
        [], [bwd, grad, use, table, first, second], smem=[top],
    )
    gh_outer, partial = kernel_call(
        outer_kernel,
        [((2, *row), BF16), ((row_count * share, CH), BF16)],
        [((2, 4, *wide), BF16)],
        "outer", 8 * row_flops,
        [], [table, first, near, below, fric, flip, sums],
    )
    partial, above = lax.optimization_barrier((partial, above))
    shares = spread_out(partial)

    fwd, gh_outer = lax.optimization_barrier((fwd, gh_outer))
    (result,) = kernel_call(
        forward_kernel,
        [((LOCAL, *row), BF16)],
        [((LOCAL, *row), BF16), ((12, *wide), BF16), ((10, *wide), BF16), ((16, COLS), F32)],
        "forward", 18 * row_flops,
        [], [fwd, use, table, first, second, above, below],
    )
    handed_act = lax.ppermute(result, "pipe", [(i, i + 1) for i in range(sections - 1)])
    (grad_x,) = kernel_call(
        grad_x_kernel,
        [((LOCAL, *row), BF16)],
        [((LOCAL, *row), BF16), ((10, *wide), BF16), ((2, 4, *wide), BF16), (weight, BF16)],
        "grad_x", 12 * row_flops,
        [], [use, grad, first, table, gh_inner, gh_outer, near, above, flip],
    )
    handed_grad = lax.ppermute(grad_x, "pipe", [(i + 1, i) for i in range(sections - 1)])
    handed_act, handed_grad = kernel_call(
        turn_kernel, [(cells, BF16)] * 2, [], "turn", 0, [], [handed_act, handed_grad]
    )
    shares, result, grad_x = lax.optimization_barrier((shares, result, grad_x))

    pairs = (row_count // 2, 2 * share, CH)
    (summed,) = kernel_call(
        lambda *refs: sum_kernel(scale, *refs), [(pairs, BF16)], [], "sum_shares", 0, [], [shares.reshape(pairs)]
    )
    gathered = spread_out(summed.reshape(partial.shape))
    grad_first, grad_second = kernel_call(spread_kernel, [(weight, F32)] * 2, [], "spread", 0, [], [gathered])
    return (handed_act[None], handed_grad[None], grad_first[None], grad_second[None])


def solution(mesh):
    cells = P("pipe", None, "rows", None)
    own = P("pipe", None, None)
    return jax.shard_map(
        body,
        mesh=mesh,
        in_specs=(cells, cells, cells, cells, own, own, own),
        out_specs=(cells, cells, own, own),
        check_vma=False,
    )
```
